512 devices in a mesh: seq: 32 (over z_lo, y, core), fsdp: 16 (over z_hi, x).
Axes of the slice: x: 4, y: 4, z: 16 (z_hi: 4, z_lo: 4; z = z_hi * 4 + z_lo), core: 2. Of those that a mesh axis runs over, the one named last changes fastest.
Arguments:
- tokens: bfloat16 [2048, 4608], P('seq'), may hold values from -6 to 6
- pre_gain: float32 [4608], replicated, may hold values from 0.5 to 1.5
- w_qkv: bfloat16 [4608, 8192], P('seq', 'fsdp'), may hold values from -0.1875 to 0.1875
- w_out: bfloat16 [4096, 4608], P('fsdp', 'seq'), may hold values from -0.09375 to 0.09375
- cache_keys: bfloat16 [8192, 2048], P('seq', 'fsdp'), may hold values from -48 to 48
- cache_values: bfloat16 [8192, 2048], P('seq', 'fsdp'), may hold values from -12 to 12
- cache_len: int32 [1], replicated, may hold values from 4096 to 8192
Outputs:
- layer_out: bfloat16 [2048, 4608], P('seq', 'fsdp')
The draws below stay inside these ranges and needn't reach their ends.
All inputs are finite; a program needn't handle non-finite values.
Results may differ from the reference program's by a relative error of at most 0.013.
The reference program's roundings to bfloat16 on the way count: a program that leaves them out, or rounds other values in their place, can miss the bound.
Values may be sent and summed in bfloat16 or wider, within the bound.
No kernel may reach another device: no remote copies, remote signals or barrier semaphores. Data moves between devices by JAX's collectives and lax.ppermute only.
A program may use at most 64 MiB of HBM per device.

```python
import jax
import jax.numpy as jnp
from jax import lax

D = 4608
HEAD = 128
TOK_DEV = 64
PRE_DEV = 256
KV_HEADS = 16
HEADS = 32
NEW_ROWS = 2048
PREFIX = 8192
N_SEQ = 32


def draw_cache_keys(key, part):
    key = jax.random.fold_in(key, 11)
    base_key = jax.random.fold_in(key, 0)
    shape = (PREFIX, KV_HEADS * HEAD)
    values = jnp.clip(1.5 * jax.random.normal(base_key, shape, jnp.float32), -9.0, 9.0)
    return values.astype(jnp.bfloat16)


def steps_of(own_key, dims, pieces, low, top_value):
    def one(dim, blocks):
        steps = jax.random.uniform(jax.random.fold_in(jax.random.fold_in(own_key, 6), dim), (blocks,), jnp.float32, low / len(pieces), top_value / len(pieces))
        return jnp.repeat(jnp.exp(steps), dims[dim] // blocks).reshape((-1,) + (1,) * (len(dims) - dim - 1))

    loudness = one(*pieces[0])
    for cut in pieces[1:]:
        loudness = loudness * one(*cut)
    return loudness


def normal_values(rng, dims, scale, most, shards=(), kind=jnp.bfloat16):
    values = scale * jax.random.normal(rng, dims, jnp.float32)
    if shards:
        values = values * steps_of(rng, dims, shards, -0.22, 0.18)
    return jnp.clip(values, -most, most).astype(kind)


def setup_inputs(seed: int = 0) -> dict:
    streams_of = jax.random.split(jax.random.key(seed), 8)
    tokens = normal_values(streams_of[0], (NEW_ROWS, D), 1.0, 6.0, ((0, 32),))
    pre_gain = jnp.clip(1.0 + 0.1 * jax.random.normal(streams_of[1], (D,), jnp.float32), 0.5, 1.5)
    w_qkv = normal_values(streams_of[2], (D, KV_HEADS * 4 * HEAD), (D // 4) ** -0.5, 0.1875, ((0, 32), (1, 16)))
    w_out = normal_values(streams_of[3], (HEADS * HEAD, D), (HEADS * HEAD) ** -0.5, 0.09375, ((0, 16), (1, 32)))
    cache_keys = draw_cache_keys(jax.random.fold_in(streams_of[7], 71), 0)
    cache_values = normal_values(streams_of[5], (PREFIX, KV_HEADS * HEAD), 2.0, 12.0, ((0, 32), (1, 16)))
    cache_len = jax.random.randint(streams_of[6], (1,), PREFIX // 2, PREFIX + 1).astype(jnp.int32)
    return dict(tokens=tokens, pre_gain=pre_gain, w_qkv=w_qkv, w_out=w_out, cache_keys=cache_keys, cache_values=cache_values, cache_len=cache_len)


masked_score = -1e+30
epsilon = 1e-06

def rotate(values, positions):
    half_dim = values.shape[-1] // 2
    inverse_freq = 10000.0 ** (-jnp.arange(half_dim, dtype=jnp.float32) / half_dim)
    angles = positions.astype(jnp.float32)[:, None] * inverse_freq[None, :]
    target = (values.shape[0],) + (1,) * (values.ndim - 2) + (half_dim,)
    cosine = jnp.cos(angles).reshape(target)
    sine_part = jnp.sin(angles).reshape(target)
    first = values[..., :half_dim]
    second = values[..., half_dim:]
    return jnp.concatenate([first * cosine - second * sine_part, second * cosine + first * sine_part], axis=-1)

def attend(queries, keys, values, allowed):
    mask = allowed[:, None, None, :]
    scores = jnp.einsum('qngh,knh->qngk', queries.astype(jnp.float32), keys.astype(jnp.float32))
    scores = jnp.where(mask, scores, masked_score)
    best = lax.optimization_barrier(jnp.max(scores, axis=-1))
    weights = jnp.where(mask, jnp.exp(scores - best[..., None]), 0.0)
    weight_sum = lax.optimization_barrier(jnp.sum(weights, axis=-1))
    rounded = lax.optimization_barrier(weights.astype(jnp.bfloat16))
    numer = jnp.einsum('qngk,knh->qngh', rounded.astype(jnp.float32), values.astype(jnp.float32))
    safe_sum = jnp.where(weight_sum > 0.0, weight_sum, 1.0)
    shares = (numer / safe_sum[..., None]).astype(jnp.bfloat16)
    return (best, weight_sum, shares)

def merge(carry_state, best, weight_sum, shares):
    running, denom, accum = carry_state
    highest = jnp.maximum(running, lax.optimization_barrier(jnp.max(best, axis=1)))
    scale_old = jnp.exp(running - highest)
    weight = weight_sum * jnp.exp(best - highest[:, None])
    denom = denom * scale_old + lax.optimization_barrier(jnp.sum(weight, axis=1))
    accum = accum * scale_old[..., None] + lax.optimization_barrier(jnp.sum(weight[..., None] * shares.astype(jnp.float32), axis=1))
    return (highest, denom, accum)

def reference(tokens, pre_gain, w_qkv, w_out, cache_keys, cache_values, cache_len):
    length = cache_len[0]
    hidden = tokens.astype(jnp.float32)
    normed = (hidden * lax.rsqrt(lax.optimization_barrier(jnp.mean(hidden * hidden, axis=-1, keepdims=True)) + epsilon) * pre_gain.astype(jnp.float32)).astype(jnp.bfloat16)
    projected = jnp.dot(normed, w_qkv, preferred_element_type=jnp.float32).reshape(NEW_ROWS, KV_HEADS, 4, HEAD)
    positions = length + jnp.arange(NEW_ROWS, dtype=jnp.int32)
    queries = (rotate(projected[:, :, 0:2], positions) * (D // HEADS) ** (-0.5)).astype(jnp.bfloat16)
    new_keys = rotate(projected[:, :, 2], positions).astype(jnp.bfloat16)
    new_values = projected[:, :, 3].astype(jnp.bfloat16)
    old_keys = cache_keys.reshape(PREFIX, KV_HEADS, HEAD)
    old_values = cache_values.reshape(PREFIX, KV_HEADS, HEAD)
    query_index = jnp.arange(NEW_ROWS, dtype=jnp.int32)

    def one_head(items):
        head_queries, key_cache, value_cache, key_new, value_new = items
        start_state = (jnp.full((NEW_ROWS, 1, 2), masked_score, jnp.float32), jnp.zeros((NEW_ROWS, 1, 2), jnp.float32), jnp.zeros((NEW_ROWS, 1, 2, HEAD), jnp.float32))

        def prefix_step(carry_state, block_index):
            offset = (block_index * PRE_DEV).astype(jnp.int32)
            block_keys = lax.dynamic_slice_in_dim(key_cache, offset, PRE_DEV, 0)
            block_values = lax.dynamic_slice_in_dim(value_cache, offset, PRE_DEV, 0)
            slot_index = offset + jnp.arange(PRE_DEV, dtype=jnp.int32)
            allowed = jnp.broadcast_to((slot_index < length)[None, :], (NEW_ROWS, PRE_DEV))
            best, weight_sum, shares = attend(head_queries, block_keys, block_values, allowed)
            return (merge(carry_state, best[:, None], weight_sum[:, None], shares[:, None]), None)

        def new_step(carry_state, block_index):
            offset = (block_index * TOK_DEV).astype(jnp.int32)
            block_keys = lax.dynamic_slice_in_dim(key_new, offset, TOK_DEV, 0)
            block_values = lax.dynamic_slice_in_dim(value_new, offset, TOK_DEV, 0)
            slot_index = offset + jnp.arange(TOK_DEV, dtype=jnp.int32)
            allowed = slot_index[None, :] <= query_index[:, None]
            best, weight_sum, shares = attend(head_queries, block_keys, block_values, allowed)
            return (merge(carry_state, best[:, None], weight_sum[:, None], shares[:, None]), None)
        carry_state, _ = lax.scan(prefix_step, start_state, jnp.arange(N_SEQ, dtype=jnp.int32))
        carry_state, _ = lax.scan(new_step, carry_state, jnp.arange(N_SEQ, dtype=jnp.int32))
        return (carry_state[2] / carry_state[1][..., None]).astype(jnp.bfloat16)
    items = (jnp.transpose(queries, (1, 0, 2, 3))[:, :, None], jnp.transpose(old_keys, (1, 0, 2))[:, :, None], jnp.transpose(old_values, (1, 0, 2))[:, :, None], jnp.transpose(new_keys, (1, 0, 2))[:, :, None], jnp.transpose(new_values, (1, 0, 2))[:, :, None])
    heads_out = lax.map(one_head, items)
    attention = jnp.transpose(heads_out, (1, 0, 2, 3, 4)).reshape(NEW_ROWS, KV_HEADS * 2 * HEAD)
    output_terms = jnp.dot(attention, w_out, preferred_element_type=jnp.float32)
    return (hidden + output_terms).astype(jnp.bfloat16)
```

```python
import jax
import jax.numpy as jnp
from jax import lax
from jax.experimental import pallas as pl
from jax.experimental.pallas import tpu as pltpu
from jax.sharding import Mesh, PartitionSpec as P

D = 4608
HEAD = 128
HEADS = 32
NZ, NY, NC, NW, NX = 4, 4, 2, 4, 4
SEQ = ("z", "y", "c")
FSDP = ("w", "x")

masked_score = -1e30
epsilon = 1e-06
VMEM_BYTES = 40 * 1024 * 1024


def rotate(values, cosine, sine_part):
    half_dim = values.shape[-1] // 2
    first = values[..., :half_dim]
    second = values[..., half_dim:]
    return jnp.concatenate(
        [first * cosine - second * sine_part, second * cosine + first * sine_part], axis=-1
    )


def copies(x, count):
    return jnp.broadcast_to(x[None], (count,) + x.shape)


def exchange(x, axis):
    return lax.all_to_all(x, axis, 0, 0, tiled=True)


def swap_core(x):
    return lax.ppermute(x, "c", [(0, 1), (1, 0)])


def block_result(query, keys, values, allowed):
    scores = lax.dot_general(
        query, keys, (((1,), (1,)), ((), ())), preferred_element_type=jnp.float32
    )
    scores = jnp.where(allowed, scores, masked_score)
    best = jnp.max(scores, axis=-1, keepdims=True)
    weights = jnp.where(allowed, jnp.exp(scores - best), 0.0)
    total = jnp.sum(weights, axis=-1, keepdims=True)
    numer = jnp.dot(weights.astype(jnp.bfloat16), values, preferred_element_type=jnp.float32)
    safe = jnp.where(total > 0.0, total, 1.0)
    share = (numer / safe).astype(jnp.bfloat16)
    return best, total, share


def combine(parts):
    highest = parts[0][0]
    for best, _, _ in parts[1:]:
        highest = jnp.maximum(highest, best)
    denom = 0.0
    accum = 0.0
    for best, total, share in parts:
        factor = jnp.exp(best - highest)
        weight = total * factor
        denom = denom + weight
        accum = accum + weight * share.astype(jnp.float32)
    return highest, denom, accum


def pack_stats(columns):
    rows = columns[0].shape[0]
    lane = lax.broadcasted_iota(jnp.int32, (rows, 128), 1)
    out = jnp.zeros((rows, 128), jnp.float32)
    for i, column in enumerate(columns):
        out = jnp.where(lane == i, column, out)
    return out


ROWS = 128


def prefix_kernel(meta, q_ref, own_ref, other_ref, out_ref):
    length, y, c = meta[0], meta[2], meta[3]
    slots = own_ref.shape[1]
    lane = lax.broadcasted_iota(jnp.int32, (ROWS, slots), 1)
    for chunk in range(q_ref.shape[0] // ROWS):
        rows = slice(chunk * ROWS, (chunk + 1) * ROWS)
        columns = []
        for head in range(2):
            query = q_ref[rows, head * HEAD : (head + 1) * HEAD]
            parts = []
            for source, core in ((own_ref, c), (other_ref, 1 - c)):
                for z in range(NZ):
                    start = ((z * NY + y) * NC + core) * slots
                    parts.append(
                        block_result(
                            query, source[z, :, :HEAD], source[z, :, HEAD:], lane < length - start
                        )
                    )
            highest, denom, accum = combine(parts)
            out_ref[rows, head * HEAD : (head + 1) * HEAD] = accum
            columns += [highest, denom]
        out_ref[rows, 2 * HEAD :] = pack_stats(columns)


def new_kernel(meta, q_ref, own_ref, other_ref, state_ref, out_ref):
    my_z, y, c = meta[1], meta[2], meta[3]
    slots = own_ref.shape[1]
    lane = lax.broadcasted_iota(jnp.int32, (ROWS, slots), 1)
    row = lax.broadcasted_iota(jnp.int32, (ROWS, slots), 0)
    for chunk in range(q_ref.shape[0] // ROWS):
        rows = slice(chunk * ROWS, (chunk + 1) * ROWS)
        row_y = (chunk * ROWS + row) // slots
        token = ((my_z * NY + row_y) * NC + c) * slots + row % slots
        offset = token - lane
        columns = []
        for head in range(2):
            lanes = slice(head * HEAD, (head + 1) * HEAD)
            query = q_ref[rows, lanes]
            parts = []
            for source, core in ((own_ref, c), (other_ref, 1 - c)):
                for z in range(NZ):
                    start = ((z * NY + y) * NC + core) * slots
                    parts.append(
                        block_result(
                            query, source[z, :, :HEAD], source[z, :, HEAD:], offset >= start
                        )
                    )
            highest, denom, accum = combine(parts)
            old_highest = state_ref[rows, 2 * HEAD + 2 * head : 2 * HEAD + 2 * head + 1]
            old_denom = state_ref[rows, 2 * HEAD + 2 * head + 1 : 2 * HEAD + 2 * head + 2]
            both = jnp.maximum(highest, old_highest)
            scale = jnp.exp(highest - both)
            old_scale = jnp.exp(old_highest - both)
            out_ref[rows, lanes] = accum * scale + state_ref[rows, lanes] * old_scale
            columns += [both, denom * scale + old_denom * old_scale]
        out_ref[rows, 2 * HEAD :] = pack_stats(columns)


def merge_kernel(state_ref, out_ref):
    for head in range(2):
        lanes = slice(head * HEAD, (head + 1) * HEAD)
        at = 2 * HEAD + 2 * head
        bests = [state_ref[i, :, at : at + 1] for i in range(NY)]
        highest = bests[0]
        for best in bests[1:]:
            highest = jnp.maximum(highest, best)
        denom = 0.0
        accum = 0.0
        for i in range(NY):
            scale = jnp.exp(bests[i] - highest)
            denom = denom + state_ref[i, :, at + 1 : at + 2] * scale
            accum = accum + state_ref[i, :, lanes] * scale
        attention = (accum / denom).astype(jnp.bfloat16)
        for i in range(NW):
            out_ref[i, :, lanes] = attention


def output_kernel(att_ref, weight_ref, residual_ref, out_ref):
    total = jnp.zeros(out_ref.shape, jnp.float32)
    for w in range(NW):
        for x in range(NX):
            total = total + lax.dot_general(
                att_ref[x, w],
                weight_ref[w * NX + x],
                (((1,), (1,)), ((), ())),
                preferred_element_type=jnp.float32,
            )
    out_ref[...] = (residual_ref[...].astype(jnp.float32) + total).astype(jnp.bfloat16)


def call(kernel, shape, dtype, operands, scalars=0, flops=0):
    specs = [pl.BlockSpec(memory_space=pltpu.SMEM)] * scalars
    specs += [pl.BlockSpec(memory_space=pltpu.VMEM)] * (len(operands) - scalars)
    moved = sum(o.size * o.dtype.itemsize for o in operands)
    return pl.pallas_call(
        kernel,
        out_shape=jax.ShapeDtypeStruct(shape, dtype),
        in_specs=specs,
        out_specs=pl.BlockSpec(memory_space=pltpu.VMEM),
        compiler_params=pltpu.CompilerParams(vmem_limit_bytes=VMEM_BYTES),
        cost_estimate=pl.CostEstimate(flops=flops, bytes_accessed=moved, transcendentals=flops // 512),
    )(*operands)


def on_device(tokens, pre_gain, w_qkv, w_out, cache_keys, cache_values, cache_len):
    tok_rows = tokens.shape[0]
    k_rows = w_qkv.shape[0]
    z, y, c = (lax.axis_index(name) for name in SEQ)
    seq_index = (z * NY + y) * NC + c
    fsdp_index = lax.axis_index("w") * NX + lax.axis_index("x")
    length = cache_len[0]
    meta = jnp.stack([length, z, y, c]).astype(jnp.int32)

    moves = [
        (s * 16 + f, (2 * f + s % 2) * 16 + s // 2) for s in range(32) for f in range(16)
    ]
    out_block = lax.ppermute(w_out.T, SEQ + FSDP, moves)
    out_weights = lax.all_gather(out_block, SEQ, axis=0, tiled=True)
    out_weights = out_weights.reshape(NW * NX, -1, 2 * HEAD)

    hidden = tokens.astype(jnp.float32)
    normed = (
        hidden * lax.rsqrt(jnp.mean(hidden * hidden, axis=-1, keepdims=True) + epsilon) * pre_gain
    ).astype(jnp.bfloat16)
    pieces = normed.reshape(tok_rows, NZ, NY, NC, k_rows).transpose(3, 2, 0, 1, 4)
    pieces = pieces.reshape(NC, NY, tok_rows, NZ * k_rows)
    pieces = jnp.where(c == 0, pieces, pieces[::-1])
    sent = pieces.transpose(1, 0, 2, 3)
    rows_in = exchange(sent, "y")
    w_own = exchange(copies(w_qkv, NZ), "z").reshape(NZ * k_rows, -1)
    w_other = swap_core(w_own)
    cache = jnp.concatenate([cache_keys, cache_values], axis=1)
    cache_own = exchange(copies(cache, NZ), "z")
    cache_other = swap_core(cache_own)

    rows_own = rows_in[:, 0].reshape(NY * tok_rows, -1)
    rows_other = rows_in[:, 1].reshape(NY * tok_rows, -1)
    partial = jnp.dot(rows_own, w_own, preferred_element_type=jnp.float32) + jnp.dot(
        rows_other, w_other, preferred_element_type=jnp.float32
    )
    partial = exchange(partial.reshape(NY, tok_rows, -1), "y")
    projected = jnp.sum(partial, axis=0)

    half_dim = HEAD // 2
    inverse_freq = 10000.0 ** (-jnp.arange(half_dim, dtype=jnp.float32) / half_dim)
    positions = length + seq_index * tok_rows + jnp.arange(tok_rows, dtype=jnp.int32)
    angles = positions.astype(jnp.float32)[:, None] * inverse_freq[None, :]
    cosine, sine_part = jnp.cos(angles), jnp.sin(angles)
    heads = [projected[:, i * HEAD : (i + 1) * HEAD] for i in range(4)]
    scale = (D // HEADS) ** (-0.5)
    queries = jnp.concatenate(
        [rotate(heads[0], cosine, sine_part) * scale, rotate(heads[1], cosine, sine_part) * scale],
        axis=1,
    ).astype(jnp.bfloat16)
    new = jnp.concatenate([rotate(heads[2], cosine, sine_part), heads[3]], axis=1).astype(
        jnp.bfloat16
    )
    all_queries = exchange(copies(queries, NY), "y").reshape(NY * tok_rows, -1)
    new_own = exchange(copies(new, NZ), "z")
    new_other = swap_core(new_own)

    state_shape = (NY * tok_rows, 3 * HEAD)
    state = call(
        prefix_kernel,
        state_shape,
        jnp.float32,
        (meta, all_queries, cache_own, cache_other),
        scalars=1,
        flops=4 * 512 * 2048 * 128,
    )
    state = call(
        new_kernel,
        state_shape,
        jnp.float32,
        (meta, all_queries, new_own, new_other, state),
        scalars=1,
        flops=4 * 512 * 512 * 128,
    )
    states = exchange(state.reshape(NY, tok_rows, -1), "y")
    attention = call(merge_kernel, (NW, tok_rows, 2 * HEAD), jnp.bfloat16, (states,))
    attention = exchange(attention, "w")
    attention = exchange(copies(attention, NX), "x")
    width = D // (NW * NX)
    residual = lax.dynamic_slice_in_dim(tokens, fsdp_index * width, width, 1)
    return call(
        output_kernel,
        (tok_rows, width),
        jnp.bfloat16,
        (attention, out_weights, residual),
        flops=2 * 64 * 4096 * 288,
    )


def solution(mesh):
    fine = Mesh(mesh.devices.reshape(NZ, NY, NC, NW, NX), SEQ + FSDP)
    return jax.shard_map(
        on_device,
        mesh=fine,
        in_specs=(
            P(SEQ, None),
            P(),
            P(SEQ, FSDP),
            P(FSDP, SEQ),
            P(SEQ, FSDP),
            P(SEQ, FSDP),
            P(),
        ),
        out_specs=P(SEQ, FSDP),
        check_vma=False,
    )
```

```python
import jax
import jax.numpy as jnp
from jax import lax
from jax.experimental import pallas as pl
from jax.experimental.pallas import tpu as pltpu
from jax.sharding import Mesh, PartitionSpec as P

D = 4608
HEAD = 128
HEADS = 32
NZ, NY, NC, NW, NX = 4, 4, 2, 4, 4
SEQ = ("z", "y", "c")
FSDP = ("w", "x")

masked_score = -1e30
epsilon = 1e-06
VMEM_BYTES = 40 * 1024 * 1024


def exchange(x, axis):
    return lax.all_to_all(x, axis, 0, 0, tiled=True)


def swap_core(x):
    return lax.ppermute(x, "c", [(0, 1), (1, 0)])


def block_result(query, keys, values, allowed):
    scores = lax.dot_general(
        query, keys, (((1,), (1,)), ((), ())), preferred_element_type=jnp.float32
    )
    scores = jnp.where(allowed, scores, masked_score)
    best = jnp.max(scores, axis=-1, keepdims=True)
    weights = jnp.exp(scores - best)
    total = jnp.where(best > 0.5 * masked_score, jnp.sum(weights, axis=-1, keepdims=True), 0.0)
    numer = jnp.dot(weights.astype(jnp.bfloat16), values, preferred_element_type=jnp.float32)
    inverse = 1.0 / jnp.where(total > 0.0, total, 1.0)
    share = (numer * inverse).astype(jnp.bfloat16)
    return best, total, share


def combine(parts):
    highest = parts[0][0]
    for best, _, _ in parts[1:]:
        highest = jnp.maximum(highest, best)
    denom = 0.0
    accum = 0.0
    for best, total, share in parts:
        weight = total * jnp.exp(best - highest)
        denom = denom + weight
        accum = accum + weight * share.astype(jnp.float32)
    return highest, denom, accum


def pack_stats(columns):
    rows = columns[0].shape[0]
    lane = lax.broadcasted_iota(jnp.int32, (rows, 128), 1)
    out = jnp.zeros((rows, 128), jnp.float32)
    for i, column in enumerate(columns):
        out = jnp.where(lane == i, column, out)
    return out


def norm_kernel(meta, tokens_ref, gain_ref, out_ref):
    hidden = tokens_ref[...].astype(jnp.float32)
    mean = jnp.mean(hidden * hidden, axis=-1, keepdims=True)
    normed = (hidden * lax.rsqrt(mean + epsilon) * gain_ref[...]).astype(jnp.bfloat16)
    first = meta[3] == 0
    k_rows = normed.shape[1] // (NZ * NY * NC)
    for y in range(NY):
        for z in range(NZ):
            at = (z * NY + y) * NC * k_rows
            low, high = normed[:, at : at + k_rows], normed[:, at + k_rows : at + 2 * k_rows]
            out_ref[y, 0, :, z * k_rows : (z + 1) * k_rows] = jnp.where(first, low, high)
            out_ref[y, 1, :, z * k_rows : (z + 1) * k_rows] = jnp.where(first, high, low)


def rotary_kernel(part_ref, cos_ref, sin_ref, q_ref, new_ref):
    total = (part_ref[0] + part_ref[1]) + (part_ref[2] + part_ref[3])
    cosine, sine_part = cos_ref[...], sin_ref[...]

    def rotated(i):
        u = total[:, i * HEAD : (i + 1) * HEAD]
        return u * cosine + pltpu.roll(u, HEAD // 2, 1) * sine_part

    scale = (D // HEADS) ** (-0.5)
    q_ref[:, :HEAD] = (rotated(0) * scale).astype(jnp.bfloat16)
    q_ref[:, HEAD:] = (rotated(1) * scale).astype(jnp.bfloat16)
    keys = rotated(2).astype(jnp.bfloat16)
    values = total[:, 3 * HEAD :].astype(jnp.bfloat16)
    for i in range(NZ):
        new_ref[i, :, :HEAD] = keys
        new_ref[i, :, HEAD:] = values


def prefix_kernel(meta, q0, q1, q2, q3, own_ref, other_ref, out_ref):
    length, y, c = meta[0], meta[2], meta[3]
    slots = own_ref.shape[1]
    rows = q0.shape[0]
    lane = lax.broadcasted_iota(jnp.int32, (2 * rows, slots), 1)
    for chunk, (qa, qb) in enumerate(((q0, q1), (q2, q3))):
        columns = []
        places = [lax.rem(y + 2 * chunk + i, NY) for i in range(2)]
        for head in range(2):
            lanes = slice(head * HEAD, (head + 1) * HEAD)
            query = jnp.concatenate([qa[:, lanes], qb[:, lanes]], axis=0)
            parts = []
            for source, core in ((own_ref, c), (other_ref, 1 - c)):
                for z in range(NZ):
                    start = ((z * NY + y) * NC + core) * slots
                    parts.append(
                        block_result(
                            query, source[z, :, :HEAD], source[z, :, HEAD:], lane < length - start
                        )
                    )
            highest, denom, accum = combine(parts)
            for i, place in enumerate(places):
                out_ref[place, :, lanes] = accum[i * rows : (i + 1) * rows]
            columns += [highest, denom]
        stats = pack_stats(columns)
        for i, place in enumerate(places):
            out_ref[place, :, 2 * HEAD :] = stats[i * rows : (i + 1) * rows]


def new_kernel(meta, q0, q1, q2, q3, own_ref, other_ref, state_ref, out_ref):
    my_z, y, c = meta[1], meta[2], meta[3]
    slots = own_ref.shape[1]
    rows = q0.shape[0]
    lane = lax.broadcasted_iota(jnp.int32, (2 * rows, slots), 1)
    row = lax.broadcasted_iota(jnp.int32, (2 * rows, slots), 0)
    for chunk, (qa, qb) in enumerate(((q0, q1), (q2, q3))):
        columns = []
        places = [lax.rem(y + 2 * chunk + i, NY) for i in range(2)]
        bases = [((my_z * NY + place) * NC + c) * slots for place in places]
        offset = jnp.where(row < rows, bases[0] + row, bases[1] + row - rows) - lane
        old_stats = jnp.concatenate([state_ref[place, :, 2 * HEAD :] for place in places], axis=0)
        for head in range(2):
            lanes = slice(head * HEAD, (head + 1) * HEAD)
            query = jnp.concatenate([qa[:, lanes], qb[:, lanes]], axis=0)
            parts = []
            for source, core in ((own_ref, c), (other_ref, 1 - c)):
                for z in range(NZ):
                    start = ((z * NY + y) * NC + core) * slots
                    parts.append(
                        block_result(
                            query, source[z, :, :HEAD], source[z, :, HEAD:], offset >= start
                        )
                    )
            highest, denom, accum = combine(parts)
            old_highest = old_stats[:, 2 * head : 2 * head + 1]
            old_denom = old_stats[:, 2 * head + 1 : 2 * head + 2]
            both = jnp.maximum(highest, old_highest)
            scale = jnp.exp(highest - both)
            old_scale = jnp.exp(old_highest - both)
            accum = accum * scale
            for i, place in enumerate(places):
                part = slice(i * rows, (i + 1) * rows)
                out_ref[place, :, lanes] = (
                    accum[part] + state_ref[place, :, lanes] * old_scale[part]
                )
            columns += [both, denom * scale + old_denom * old_scale]
        stats = pack_stats(columns)
        for i, place in enumerate(places):
            out_ref[place, :, 2 * HEAD :] = stats[i * rows : (i + 1) * rows]


def merge_kernel(state_ref, out_ref):
    for head in range(2):
        lanes = slice(head * HEAD, (head + 1) * HEAD)
        at = 2 * HEAD + 2 * head
        bests = [state_ref[i, :, at : at + 1] for i in range(NY)]
        highest = bests[0]
        for best in bests[1:]:
            highest = jnp.maximum(highest, best)
        denom = 0.0
        accum = 0.0
        for i in range(NY):
            scale = jnp.exp(bests[i] - highest)
            denom = denom + state_ref[i, :, at + 1 : at + 2] * scale
            accum = accum + state_ref[i, :, lanes] * scale
        attention = (accum / denom).astype(jnp.bfloat16)
        for i in range(NW):
            out_ref[i, :, lanes] = attention


def output_kernel(meta, att_ref, own_ref, other_ref, out_ref):
    first = meta[3] == 0
    half = own_ref.shape[2]
    for x in range(NX):
        sums = []
        for source in (own_ref, other_ref):
            total = 0.0
            for w in range(NW):
                total = total + lax.dot_general(
                    att_ref[w],
                    source[x, w],
                    (((1,), (1,)), ((), ())),
                    preferred_element_type=jnp.float32,
                )
            sums.append(total)
        out_ref[x, :, :half] = jnp.where(first, sums[0], sums[1])
        out_ref[x, :, half:] = jnp.where(first, sums[1], sums[0])


def last_kernel(part_ref, residual_ref, out_ref):
    total = (part_ref[0] + part_ref[1]) + (part_ref[2] + part_ref[3])
    out_ref[...] = (residual_ref[...].astype(jnp.float32) + total).astype(jnp.bfloat16)


def call(kernel, out, operands, scalars=0, flops=0):
    specs = [pl.BlockSpec(memory_space=pltpu.SMEM)] * scalars
    specs += [pl.BlockSpec(memory_space=pltpu.VMEM)] * (len(operands) - scalars)
    moved = sum(o.size * o.dtype.itemsize for o in operands)
    shapes = [jax.ShapeDtypeStruct(shape, dtype) for shape, dtype in out]
    results = pl.pallas_call(
        kernel,
        out_shape=shapes,
        in_specs=specs,
        out_specs=[pl.BlockSpec(memory_space=pltpu.VMEM)] * len(out),
        compiler_params=pltpu.CompilerParams(vmem_limit_bytes=VMEM_BYTES),
        cost_estimate=pl.CostEstimate(
            flops=flops, bytes_accessed=moved, transcendentals=flops // 512
        ),
    )(*operands)
    return results if len(out) > 1 else results[0]


def on_device(tokens, pre_gain, w_qkv, w_out, cache_keys, cache_values, cache_len):
    tok_rows = tokens.shape[0]
    k_rows = w_qkv.shape[0]
    bf16, f32 = jnp.bfloat16, jnp.float32
    z, y, c = (lax.axis_index(name) for name in SEQ)
    seq_index = (z * NY + y) * NC + c
    fsdp_index = lax.axis_index("w") * NX + lax.axis_index("x")
    length = cache_len[0]
    meta = jnp.stack([length, z, y, c]).astype(jnp.int32)

    w_own = lax.all_gather(w_qkv, "z", axis=0, tiled=True)
    w_other = swap_core(w_own)
    cache = jnp.concatenate([cache_keys, cache_values], axis=1)
    cache_own = lax.all_gather(cache, "z", axis=0)
    cache_other = swap_core(cache_own)
    trade = [(a * NW + b, b * NW + a) for a in range(NZ) for b in range(NW)]
    out_block = lax.ppermute(w_out.T, ("z", "w"), trade)
    out_block = lax.all_gather(out_block, "z", axis=0)
    out_own = lax.all_gather(out_block, "y", axis=0)
    out_other = swap_core(out_own)

    rows_out = call(
        norm_kernel,
        [((NY, NC, tok_rows, NZ * k_rows), bf16)],
        (meta, tokens, pre_gain.reshape(1, -1)),
        scalars=1,
        flops=tokens.size * 6,
    )
    rows_in = exchange(rows_out, "y")
    rows_own = rows_in[:, 0].reshape(NY * tok_rows, -1)
    rows_other = rows_in[:, 1].reshape(NY * tok_rows, -1)
    partial = jnp.dot(rows_own, w_own, preferred_element_type=f32) + jnp.dot(
        rows_other, w_other, preferred_element_type=f32
    )
    partial = exchange(partial.reshape(NY, tok_rows, -1), "y")

    half_dim = HEAD // 2
    inverse_freq = 10000.0 ** (-jnp.arange(half_dim, dtype=f32) / half_dim)
    positions = length + seq_index * tok_rows + jnp.arange(tok_rows, dtype=jnp.int32)
    angles = positions.astype(f32)[:, None] * inverse_freq[None, :]
    cosine, sine_part = jnp.cos(angles), jnp.sin(angles)
    cosine = jnp.concatenate([cosine, cosine], axis=1)
    sine_part = jnp.concatenate([-sine_part, sine_part], axis=1)
    queries, new = call(
        rotary_kernel,
        [((tok_rows, 2 * HEAD), bf16), ((NZ, tok_rows, 2 * HEAD), bf16)],
        (partial, cosine, sine_part),
    )
    new_own = exchange(new, "z")
    new_other = swap_core(new_own)
    all_queries = [queries] + [
        lax.ppermute(queries, "y", [((i + k) % NY, i) for i in range(NY)]) for k in range(1, NY)
    ]

    state_shape = [((NY, tok_rows, 3 * HEAD), f32)]
    state = call(
        prefix_kernel,
        state_shape,
        (meta, *all_queries, cache_own, cache_other),
        scalars=1,
        flops=4 * 512 * 2048 * 128,
    )
    state = call(
        new_kernel,
        state_shape,
        (meta, *all_queries, new_own, new_other, state),
        scalars=1,
        flops=4 * 512 * 512 * 128,
    )
    states = exchange(state, "y")
    attention = call(merge_kernel, [((NW, tok_rows, 2 * HEAD), bf16)], (states,))
    attention = exchange(attention, "w")
    width = D // (NW * NX)
    terms = call(
        output_kernel,
        [((NX, tok_rows, width), f32)],
        (meta, attention, out_own, out_other),
        scalars=1,
        flops=2 * 64 * 4096 * 288,
    )
    terms = exchange(terms, "x")
    residual = lax.dynamic_slice_in_dim(tokens, fsdp_index * width, width, 1)
    return call(last_kernel, [((tok_rows, width), bf16)], (terms, residual))


def solution(mesh):
    fine = Mesh(mesh.devices.reshape(NZ, NY, NC, NW, NX), SEQ + FSDP)
    return jax.shard_map(
        on_device,
        mesh=fine,
        in_specs=(
            P(SEQ, None),
            P(),
            P(SEQ, FSDP),
            P(FSDP, SEQ),
            P(SEQ, FSDP),
            P(SEQ, FSDP),
            P(),
        ),
        out_specs=P(SEQ, FSDP),
        check_vma=False,
    )
```

```python
import jax
import jax.numpy as jnp
from jax import lax
from jax.experimental import pallas as pl
from jax.experimental.pallas import tpu as pltpu
from jax.sharding import Mesh, PartitionSpec as P

D = 4608
HEAD = 128
HEADS = 32
NZ, NY, NC, NW, NX = 4, 4, 2, 4, 4
SEQ = ("z", "y", "c")
FSDP = ("w", "x")

masked_score = -1e30
epsilon = 1e-06
VMEM_BYTES = 40 * 1024 * 1024


def exchange(x, axis):
    return lax.all_to_all(x, axis, 0, 0, tiled=True)


def from_next(x, axis, step, size):
    return lax.ppermute(x, axis, [((i + step) % size, i) for i in range(size)])


def from_pair(x, axis, bit, size):
    return lax.ppermute(x, axis, [(i ^ bit, i) for i in range(size)])


def gather_z(x):
    pair = jnp.stack([x, from_pair(x, "z", 1, NZ)])
    return jnp.concatenate([pair, from_pair(pair, "z", 2, NZ)])


def gather_y(x):
    after, before = from_next(x, "y", 1, NY), from_next(x, "y", NY - 1, NY)
    half = x.shape[0] // 2
    low = from_next(after[:half], "y", 1, NY)
    high = from_next(before[half:], "y", NY - 1, NY)
    return jnp.stack([x, after, jnp.concatenate([low, high]), before])


def swap_core(x):
    return lax.ppermute(x, "c", [(0, 1), (1, 0)])


def block_result(query, keys, values, allowed):
    scores = lax.dot_general(
        query, keys, (((1,), (1,)), ((), ())), preferred_element_type=jnp.float32
    )
    scores = jnp.where(allowed, scores, masked_score)
    best = jnp.max(scores, axis=-1, keepdims=True)
    weights = jnp.exp(scores - best)
    total = jnp.where(best > 0.5 * masked_score, jnp.sum(weights, axis=-1, keepdims=True), 0.0)
    numer = jnp.dot(weights.astype(jnp.bfloat16), values, preferred_element_type=jnp.float32)
    inverse = 1.0 / jnp.where(total > 0.0, total, 1.0)
    share = (numer * inverse).astype(jnp.bfloat16)
    return best, total, share


def combine(parts):
    highest = parts[0][0]
    for best, _, _ in parts[1:]:
        highest = jnp.maximum(highest, best)
    denom = 0.0
    accum = 0.0
    for best, total, share in parts:
        weight = total * jnp.exp(best - highest)
        denom = denom + weight
        accum = accum + weight * share.astype(jnp.float32)
    return highest, denom, accum


def pack_stats(columns):
    rows = columns[0].shape[0]
    lane = lax.broadcasted_iota(jnp.int32, (rows, 128), 1)
    out = jnp.zeros((rows, 128), jnp.float32)
    for i, column in enumerate(columns):
        out = jnp.where(lane == i, column, out)
    return out


def norm_kernel(meta, tokens_ref, gain_ref, out_ref, normed_ref):
    hidden = tokens_ref[...].astype(jnp.float32)
    mean = jnp.mean(hidden * hidden, axis=-1, keepdims=True)
    normed_ref[...] = (hidden * lax.rsqrt(mean + epsilon) * gain_ref[...]).astype(jnp.bfloat16)
    first = meta[3] == 0
    span = normed_ref.shape[1] // NZ
    k_rows = span // (NY * NC)
    for k in range(NZ):
        block = meta[1] ^ k
        part = normed_ref[:, pl.ds(pl.multiple_of(block * span, span), span)]
        for y in range(NY):
            at = y * NC * k_rows
            low, high = part[:, at : at + k_rows], part[:, at + k_rows : at + 2 * k_rows]
            out_ref[y, 0, :, k * k_rows : (k + 1) * k_rows] = jnp.where(first, low, high)
            out_ref[y, 1, :, k * k_rows : (k + 1) * k_rows] = jnp.where(first, high, low)


def rotary_kernel(part_ref, cos_ref, sin_ref, q_ref, new_ref):
    total = (part_ref[0] + part_ref[1]) + (part_ref[2] + part_ref[3])
    cosine, sine_part = cos_ref[...], sin_ref[...]

    def rotated(i):
        u = total[:, i * HEAD : (i + 1) * HEAD]
        return u * cosine + pltpu.roll(u, HEAD // 2, 1) * sine_part

    scale = (D // HEADS) ** (-0.5)
    q_ref[:, :HEAD] = (rotated(0) * scale).astype(jnp.bfloat16)
    q_ref[:, HEAD:] = (rotated(1) * scale).astype(jnp.bfloat16)
    keys = rotated(2).astype(jnp.bfloat16)
    values = total[:, 3 * HEAD :].astype(jnp.bfloat16)
    for i in range(NZ * NC):
        new_ref[i, :, :HEAD] = keys
        new_ref[i, :, HEAD:] = values


def prefix_kernel(meta, q0, q1, q2, q3, own_ref, other_ref, out_ref):
    length, my_z, y, c = meta[0], meta[1], meta[2], meta[3]
    slots = own_ref.shape[1]
    rows = q0.shape[0]
    lane = lax.broadcasted_iota(jnp.int32, (2 * rows, slots), 1)
    for chunk, (qa, qb) in enumerate(((q0, q1), (q2, q3))):
        columns = []
        places = [lax.rem(y + 2 * chunk + i, NY) for i in range(2)]
        for head in range(2):
            lanes = slice(head * HEAD, (head + 1) * HEAD)
            query = jnp.concatenate([qa[:, lanes], qb[:, lanes]], axis=0)
            parts = []
            for source, core in ((own_ref, c), (other_ref, 1 - c)):
                for k in range(NZ):
                    start = (((my_z ^ k) * NY + y) * NC + core) * slots
                    parts.append(
                        block_result(
                            query, source[k, :, :HEAD], source[k, :, HEAD:], lane < length - start
                        )
                    )
            highest, denom, accum = combine(parts)
            for i, place in enumerate(places):
                out_ref[place, :, lanes] = accum[i * rows : (i + 1) * rows]
            columns += [highest, denom]
        stats = pack_stats(columns)
        for i, place in enumerate(places):
            out_ref[place, :, 2 * HEAD :] = stats[i * rows : (i + 1) * rows]


def new_kernel(meta, q0, q1, q2, q3, new_ref, state_ref, out_ref):
    my_z, y, c = meta[1], meta[2], meta[3]
    slots = new_ref.shape[1]
    rows = q0.shape[0]
    lane = lax.broadcasted_iota(jnp.int32, (2 * rows, slots), 1)
    row = lax.broadcasted_iota(jnp.int32, (2 * rows, slots), 0)
    for chunk, (qa, qb) in enumerate(((q0, q1), (q2, q3))):
        columns = []
        places = [lax.rem(y + 2 * chunk + i, NY) for i in range(2)]
        bases = [((my_z * NY + place) * NC + c) * slots for place in places]
        offset = jnp.where(row < rows, bases[0] + row, bases[1] + row - rows) - lane
        old_stats = jnp.concatenate([state_ref[place, :, 2 * HEAD :] for place in places], axis=0)
        for head in range(2):
            lanes = slice(head * HEAD, (head + 1) * HEAD)
            query = jnp.concatenate([qa[:, lanes], qb[:, lanes]], axis=0)
            parts = []
            for k in range(NZ * NC):
                start = ((k // NC * NY + y) * NC + k % NC) * slots
                parts.append(
                    block_result(
                        query, new_ref[k, :, :HEAD], new_ref[k, :, HEAD:], offset >= start
                    )
                )
            highest, denom, accum = combine(parts)
            old_highest = old_stats[:, 2 * head : 2 * head + 1]
            old_denom = old_stats[:, 2 * head + 1 : 2 * head + 2]
            both = jnp.maximum(highest, old_highest)
            scale = jnp.exp(highest - both)
            old_scale = jnp.exp(old_highest - both)
            accum = accum * scale
            for i, place in enumerate(places):
                part = slice(i * rows, (i + 1) * rows)
                out_ref[place, :, lanes] = (
                    accum[part] + state_ref[place, :, lanes] * old_scale[part]
                )
            columns += [both, denom * scale + old_denom * old_scale]
        stats = pack_stats(columns)
        for i, place in enumerate(places):
            out_ref[place, :, 2 * HEAD :] = stats[i * rows : (i + 1) * rows]


def merge_kernel(state_ref, out_ref):
    for head in range(2):
        lanes = slice(head * HEAD, (head + 1) * HEAD)
        at = 2 * HEAD + 2 * head
        bests = [state_ref[i, :, at : at + 1] for i in range(NY)]
        highest = bests[0]
        for best in bests[1:]:
            highest = jnp.maximum(highest, best)
        denom = 0.0
        accum = 0.0
        for i in range(NY):
            scale = jnp.exp(bests[i] - highest)
            denom = denom + state_ref[i, :, at + 1 : at + 2] * scale
            accum = accum + state_ref[i, :, lanes] * scale
        attention = (accum / denom).astype(jnp.bfloat16)
        for i in range(NW):
            out_ref[i, :, lanes] = attention


def output_kernel(meta, att_ref, own_ref, other_ref, out_ref):
    first = meta[3] == 0
    half = own_ref.shape[2]
    for x in range(NX):
        place = lax.rem(meta[2] + x, NX)
        sums = []
        for source in (own_ref, other_ref):
            total = 0.0
            for k in range(NW):
                total = total + lax.dot_general(
                    att_ref[meta[1] ^ k],
                    source[x, k],
                    (((1,), (1,)), ((), ())),
                    preferred_element_type=jnp.float32,
                )
            sums.append(total)
        out_ref[place, :, :half] = jnp.where(first, sums[0], sums[1])
        out_ref[place, :, half:] = jnp.where(first, sums[1], sums[0])


def last_kernel(part_ref, residual_ref, out_ref):
    total = (part_ref[0] + part_ref[1]) + (part_ref[2] + part_ref[3])
    out_ref[...] = (residual_ref[...].astype(jnp.float32) + total).astype(jnp.bfloat16)


def call(kernel, out, operands, scalars=0, flops=0, scratch=()):
    specs = [pl.BlockSpec(memory_space=pltpu.SMEM)] * scalars
    specs += [pl.BlockSpec(memory_space=pltpu.VMEM)] * (len(operands) - scalars)
    moved = sum(o.size * o.dtype.itemsize for o in operands)
    shapes = [jax.ShapeDtypeStruct(shape, dtype) for shape, dtype in out]
    results = pl.pallas_call(
        kernel,
        out_shape=shapes,
        in_specs=specs,
        out_specs=[pl.BlockSpec(memory_space=pltpu.VMEM)] * len(out),
        scratch_shapes=list(scratch),
        compiler_params=pltpu.CompilerParams(vmem_limit_bytes=VMEM_BYTES),
        cost_estimate=pl.CostEstimate(
            flops=flops, bytes_accessed=moved, transcendentals=flops // 512
        ),
    )(*operands)
    return results if len(out) > 1 else results[0]


def on_device(tokens, pre_gain, w_qkv, w_out, cache_keys, cache_values, cache_len):
    tok_rows = tokens.shape[0]
    k_rows = w_qkv.shape[0]
    bf16, f32 = jnp.bfloat16, jnp.float32
    z, y, c = (lax.axis_index(name) for name in SEQ)
    seq_index = (z * NY + y) * NC + c
    fsdp_index = lax.axis_index("w") * NX + lax.axis_index("x")
    length = cache_len[0]
    meta = jnp.stack([length, z, y, c]).astype(jnp.int32)

    w_own = gather_z(w_qkv)
    w_other = swap_core(w_own)
    cache_own = gather_z(jnp.concatenate([cache_keys, cache_values], axis=1))
    cache_other = swap_core(cache_own)
    trade = [(a * NW + b, b * NW + a) for a in range(NZ) for b in range(NW)]
    out_block = lax.ppermute(w_out.T, ("z", "w"), trade)
    out_block = gather_z(out_block)
    out_own = gather_y(out_block)
    out_other = swap_core(out_own)

    rows_out = call(
        norm_kernel,
        [((NY, NC, tok_rows, NZ * k_rows), bf16)],
        (meta, tokens, pre_gain.reshape(1, -1)),
        scalars=1,
        flops=tokens.size * 6,
        scratch=[pltpu.VMEM(tokens.shape, bf16)],
    )
    rows_in = exchange(rows_out, "y")
    w_own, w_other = (w.reshape(NZ * k_rows, -1) for w in (w_own, w_other))
    rows_own = rows_in[:, 0].reshape(NY * tok_rows, -1)
    rows_other = rows_in[:, 1].reshape(NY * tok_rows, -1)
    partial = jnp.dot(rows_own, w_own, preferred_element_type=f32) + jnp.dot(
        rows_other, w_other, preferred_element_type=f32
    )
    partial = exchange(partial.reshape(NY, tok_rows, -1), "y")

    half_dim = HEAD // 2
    inverse_freq = 10000.0 ** (-jnp.arange(half_dim, dtype=f32) / half_dim)
    positions = length + seq_index * tok_rows + jnp.arange(tok_rows, dtype=jnp.int32)
    angles = positions.astype(f32)[:, None] * inverse_freq[None, :]
    cosine, sine_part = jnp.cos(angles), jnp.sin(angles)
    cosine = jnp.concatenate([cosine, cosine], axis=1)
    sine_part = jnp.concatenate([-sine_part, sine_part], axis=1)
    queries, new = call(
        rotary_kernel,
        [((tok_rows, 2 * HEAD), bf16), ((NZ * NC, tok_rows, 2 * HEAD), bf16)],
        (partial, cosine, sine_part),
    )
    all_new = exchange(new, ("z", "c"))
    all_queries = [queries] + [from_next(queries, "y", k, NY) for k in range(1, NY)]

    state_shape = [((NY, tok_rows, 3 * HEAD), f32)]
    state = call(
        prefix_kernel,
        state_shape,
        (meta, *all_queries, cache_own, cache_other),
        scalars=1,
        flops=4 * 512 * 2048 * 128,
    )
    state = call(
        new_kernel,
        state_shape,
        (meta, *all_queries, all_new, state),
        scalars=1,
        flops=4 * 512 * 512 * 128,
    )
    states = exchange(state, "y")
    attention = call(merge_kernel, [((NW, tok_rows, 2 * HEAD), bf16)], (states,))
    attention = exchange(attention, "w")
    width = D // (NW * NX)
    terms = call(
        output_kernel,
        [((NX, tok_rows, width), f32)],
        (meta, attention, out_own, out_other),
        scalars=1,
        flops=2 * 64 * 4096 * 288,
    )
    terms = exchange(terms, "x")
    residual = lax.dynamic_slice_in_dim(tokens, fsdp_index * width, width, 1)
    return call(last_kernel, [((tok_rows, width), bf16)], (terms, residual))


def solution(mesh):
    fine = Mesh(mesh.devices.reshape(NZ, NY, NC, NW, NX), SEQ + FSDP)
    return jax.shard_map(
        on_device,
        mesh=fine,
        in_specs=(
            P(SEQ, None),
            P(),
            P(SEQ, FSDP),
            P(FSDP, SEQ),
            P(SEQ, FSDP),
            P(SEQ, FSDP),
            P(),
        ),
        out_specs=P(SEQ, FSDP),
        check_vma=False,
    )
```

```python
import jax
import jax.numpy as jnp
from jax import lax
from jax.experimental import pallas as pl
from jax.experimental.pallas import tpu as pltpu
from jax.sharding import Mesh, PartitionSpec as P

D = 4608
HEAD = 128
HEADS = 32
NZ, NY, NC, NW, NX = 4, 4, 2, 4, 4
SEQ = ("z", "y", "c")
FSDP = ("w", "x")

masked_score = -1e30
epsilon = 1e-06
VMEM_BYTES = 40 * 1024 * 1024


def exchange(x, axis):
    return lax.all_to_all(x, axis, 0, 0, tiled=True)


def from_next(x, axis, step, size):
    return lax.ppermute(x, axis, [((i + step) % size, i) for i in range(size)])


def from_pair(x, axis, bit, size):
    return lax.ppermute(x, axis, [(i ^ bit, i) for i in range(size)])


def gather_y(x):
    after, before = from_next(x, "y", 1, NY), from_next(x, "y", NY - 1, NY)
    half = x.shape[0] // 2
    low = from_next(after[:half], "y", 1, NY)
    high = from_next(before[half:], "y", NY - 1, NY)
    return jnp.stack([x, after, jnp.concatenate([low, high]), before])


def swap_core(x):
    return lax.ppermute(x, "c", [(0, 1), (1, 0)])


def block_result(query, keys, values, allowed):
    scores = lax.dot_general(
        keys, query, (((1,), (1,)), ((), ())), preferred_element_type=jnp.float32
    )
    scores = jnp.where(allowed, scores, masked_score)
    best = jnp.max(scores, axis=0, keepdims=True)
    weights = jnp.exp(scores - best)
    total = jnp.where(best > 0.5 * masked_score, jnp.sum(weights, axis=0, keepdims=True), 0.0)
    numer = lax.dot_general(
        values,
        weights.astype(jnp.bfloat16),
        (((0,), (0,)), ((), ())),
        preferred_element_type=jnp.float32,
    )
    inverse = 1.0 / jnp.where(total > 0.0, total, 1.0)
    share = (numer * inverse).astype(jnp.bfloat16)
    return best, total, share


def combine(parts):
    highest = parts[0][0]
    for best, _, _ in parts[1:]:
        highest = jnp.maximum(highest, best)
    denom = 0.0
    accum = 0.0
    for best, total, share in parts:
        weight = total * jnp.exp(best - highest)
        denom = denom + weight
        accum = accum + weight * share.astype(jnp.float32)
    return highest, denom, accum


def norm_kernel(meta, tokens_ref, gain_ref, out_ref, normed_ref):
    hidden = tokens_ref[...].astype(jnp.float32)
    mean = jnp.mean(hidden * hidden, axis=-1, keepdims=True)
    normed_ref[...] = (hidden * lax.rsqrt(mean + epsilon) * gain_ref[...]).astype(jnp.bfloat16)
    first = meta[3] == 0
    span = normed_ref.shape[1] // NZ
    k_rows = span // (NY * NC)
    for k in range(NZ):
        block = meta[1] ^ k
        part = normed_ref[:, pl.ds(pl.multiple_of(block * span, span), span)]
        for y in range(NY):
            at = y * NC * k_rows
            low, high = part[:, at : at + k_rows], part[:, at + k_rows : at + 2 * k_rows]
            out_ref[y, 0, :, k * k_rows : (k + 1) * k_rows] = jnp.where(first, low, high)
            out_ref[y, 1, :, k * k_rows : (k + 1) * k_rows] = jnp.where(first, high, low)


def project_kernel(rows_ref, own_ref, other_ref, out_ref):
    own = own_ref[...].reshape(-1, own_ref.shape[2])
    other = other_ref[...].reshape(-1, other_ref.shape[2])
    peers, _, rows, depth = rows_ref.shape
    total = jnp.dot(
        rows_ref[:, 0].reshape(peers * rows, depth), own, preferred_element_type=jnp.float32
    ) + jnp.dot(
        rows_ref[:, 1].reshape(peers * rows, depth), other, preferred_element_type=jnp.float32
    )
    out_ref[...] = total.reshape(out_ref.shape)


def rotary_kernel(part_ref, cos_ref, sin_ref, q_ref, new_ref):
    total = (part_ref[0] + part_ref[1]) + (part_ref[2] + part_ref[3])
    cosine, sine_part = cos_ref[...], sin_ref[...]

    def rotated(i):
        u = total[:, i * HEAD : (i + 1) * HEAD]
        return u * cosine + pltpu.roll(u, HEAD // 2, 1) * sine_part

    scale = (D // HEADS) ** (-0.5)
    q_ref[:, :HEAD] = (rotated(0) * scale).astype(jnp.bfloat16)
    q_ref[:, HEAD:] = (rotated(1) * scale).astype(jnp.bfloat16)
    keys = rotated(2).astype(jnp.bfloat16)
    values = total[:, 3 * HEAD :].astype(jnp.bfloat16)
    for i in range(NZ * NC):
        new_ref[i, :, :HEAD] = keys
        new_ref[i, :, HEAD:] = values


def attention_kernel(meta, q0, q1, q2, q3, own_ref, other_ref, new_ref, out_ref):
    length, my_z, y, c = meta[0], meta[1], meta[2], meta[3]
    slots, new_slots = own_ref.shape[1], new_ref.shape[1]
    rows = q0.shape[0]
    lanes = 4 * rows
    slot = lax.broadcasted_iota(jnp.int32, (slots, lanes), 0)
    key = lax.broadcasted_iota(jnp.int32, (new_slots, lanes), 0)
    lane = lax.broadcasted_iota(jnp.int32, (new_slots, lanes), 1)
    for chunk, pair in enumerate(((q0, q1), (q2, q3))):
        query = jnp.concatenate(
            [q[:, h * HEAD : (h + 1) * HEAD] for q in pair for h in range(2)], axis=0
        )
        places = [lax.rem(y + 2 * chunk + i, NY) for i in range(2)]
        bases = [((my_z * NY + place) * NC + c) * rows for place in places]
        token = jnp.where(lane < 2 * rows, bases[0], bases[1]) + lane % rows
        offset = token - key
        parts = []
        for source, core in ((own_ref, c), (other_ref, 1 - c)):
            for k in range(NZ):
                start = (((my_z ^ k) * NY + y) * NC + core) * slots
                parts.append(
                    block_result(
                        query, source[k, :, :HEAD], source[k, :, HEAD:], slot < length - start
                    )
                )
        for k in range(NZ * NC):
            start = ((k // NC * NY + y) * NC + k % NC) * new_slots
            parts.append(
                block_result(query, new_ref[k, :, :HEAD], new_ref[k, :, HEAD:], offset >= start)
            )
        highest, denom, accum = combine(parts)
        row = lax.broadcasted_iota(jnp.int32, (8, 2 * rows), 0)
        for i, place in enumerate(places):
            part = slice(i * 2 * rows, (i + 1) * 2 * rows)
            out_ref[place, :HEAD, :] = accum[:, part]
            out_ref[place, HEAD:, :] = jnp.where(row == 0, highest[:, part], denom[:, part])


def merge_kernel(state_ref, out_ref):
    rows = out_ref.shape[1]
    bests = [state_ref[i, HEAD : HEAD + 1, :] for i in range(NY)]
    highest = bests[0]
    for best in bests[1:]:
        highest = jnp.maximum(highest, best)
    denom = 0.0
    accum = 0.0
    for i in range(NY):
        scale = jnp.exp(bests[i] - highest)
        denom = denom + state_ref[i, HEAD + 1 : HEAD + 2, :] * scale
        accum = accum + state_ref[i, :HEAD, :] * scale
    attention = jnp.transpose(accum / denom).astype(jnp.bfloat16)
    for i in range(NW):
        out_ref[i, :, :HEAD] = attention[:rows]
        out_ref[i, :, HEAD:] = attention[rows:]


def output_kernel(meta, att_ref, own_ref, other_ref, out_ref):
    first = meta[3] == 0
    half = own_ref.shape[2]
    for x in range(NX):
        place = lax.rem(meta[2] + x, NX)
        sums = []
        for source in (own_ref, other_ref):
            total = 0.0
            for k in range(NW):
                total = total + lax.dot_general(
                    att_ref[meta[1] ^ k],
                    source[x, k],
                    (((1,), (1,)), ((), ())),
                    preferred_element_type=jnp.float32,
                )
            sums.append(total)
        out_ref[place, :, :half] = jnp.where(first, sums[0], sums[1])
        out_ref[place, :, half:] = jnp.where(first, sums[1], sums[0])


def last_kernel(part_ref, residual_ref, out_ref):
    total = (part_ref[0] + part_ref[1]) + (part_ref[2] + part_ref[3])
    out_ref[...] = (residual_ref[...].astype(jnp.float32) + total).astype(jnp.bfloat16)


def call(kernel, out, operands, scalars=0, flops=0, scratch=(), held=()):
    count, extra = len(operands), len(held)

    def body(*refs):
        after = count + extra
        kernel(*refs[:count], *refs[after : after + len(out)], *refs[after + len(out) + extra :])

    specs = [pl.BlockSpec(memory_space=pltpu.SMEM)] * scalars
    specs += [pl.BlockSpec(memory_space=pltpu.VMEM)] * (count - scalars)
    moved = sum(o.size * o.dtype.itemsize for o in operands)
    shapes = [jax.ShapeDtypeStruct(shape, dtype) for shape, dtype in out]
    shapes += [jax.ShapeDtypeStruct(h.shape, h.dtype) for h in held]
    results = pl.pallas_call(
        body,
        out_shape=shapes,
        in_specs=specs + [pl.BlockSpec(memory_space=pl.ANY)] * extra,
        out_specs=[pl.BlockSpec(memory_space=pltpu.VMEM)] * len(out)
        + [pl.BlockSpec(memory_space=pl.ANY)] * extra,
        scratch_shapes=list(scratch),
        input_output_aliases={count + i: len(out) + i for i in range(extra)},
        compiler_params=pltpu.CompilerParams(vmem_limit_bytes=VMEM_BYTES),
        cost_estimate=pl.CostEstimate(
            flops=flops, bytes_accessed=moved, transcendentals=flops // 512
        ),
    )(*operands, *held)
    return results if len(results) > 1 else results[0]


def on_device(tokens, pre_gain, w_qkv, w_out, cache_keys, cache_values, cache_len):
    tok_rows = tokens.shape[0]
    k_rows = w_qkv.shape[0]
    bf16, f32 = jnp.bfloat16, jnp.float32
    z, y, c = (lax.axis_index(name) for name in SEQ)
    seq_index = (z * NY + y) * NC + c
    fsdp_index = lax.axis_index("w") * NX + lax.axis_index("x")
    length = cache_len[0]
    meta = jnp.stack([length, z, y, c]).astype(jnp.int32)

    w_own = jnp.stack([w_qkv] + [from_pair(w_qkv, "z", k, NZ) for k in range(1, NZ)])
    w_other = swap_core(w_own)
    cache = jnp.concatenate([cache_keys, cache_values], axis=1)
    rows_out, cache, out_block = call(
        norm_kernel,
        [((NY, NC, tok_rows, NZ * k_rows), bf16)],
        (meta, tokens, pre_gain.reshape(1, -1)),
        scalars=1,
        flops=tokens.size * 6,
        scratch=[pltpu.VMEM(tokens.shape, bf16)],
        held=(cache, w_out.T),
    )
    rows_in = exchange(rows_out, "y")
    trade = [(a * NW + b, b * NW + a) for a in range(NZ) for b in range(NW)]
    out_block = lax.ppermute(out_block, ("z", "w"), trade)
    cache = jnp.stack([cache, from_pair(cache, "z", 1, NZ)])
    partial, cache, out_block = call(
        project_kernel,
        [((NY, tok_rows, w_qkv.shape[1]), f32)],
        (rows_in, w_own, w_other),
        flops=2 * 256 * 1152 * 512,
        held=(cache, out_block),
    )
    partial = exchange(partial, "y")
    cache_own = jnp.concatenate([cache, from_pair(cache, "z", 2, NZ)])
    cache_other = swap_core(cache_own)
    out_pair = jnp.stack([out_block, from_pair(out_block, "z", 1, NZ)])

    half_dim = HEAD // 2
    inverse_freq = 10000.0 ** (-jnp.arange(half_dim, dtype=f32) / half_dim)
    positions = length + seq_index * tok_rows + jnp.arange(tok_rows, dtype=jnp.int32)
    angles = positions.astype(f32)[:, None] * inverse_freq[None, :]
    cosine, sine_part = jnp.cos(angles), jnp.sin(angles)
    cosine = jnp.concatenate([cosine, cosine], axis=1)
    sine_part = jnp.concatenate([-sine_part, sine_part], axis=1)
    queries, new, out_pair = call(
        rotary_kernel,
        [((tok_rows, 2 * HEAD), bf16), ((NZ * NC, tok_rows, 2 * HEAD), bf16)],
        (partial, cosine, sine_part),
        held=(out_pair,),
    )
    all_new = exchange(new, ("z", "c"))
    all_queries = [queries] + [from_next(queries, "y", k, NY) for k in range(1, NY)]
    out_own = gather_y(jnp.concatenate([out_pair, from_pair(out_pair, "z", 2, NZ)]))
    out_other = swap_core(out_own)

    state = call(
        attention_kernel,
        [((NY, HEAD + 8, 2 * tok_rows), f32)],
        (meta, *all_queries, cache_own, cache_other, all_new),
        scalars=1,
        flops=4 * 512 * 2560 * 128,
    )
    states = exchange(state, "y")
    attention = call(merge_kernel, [((NW, tok_rows, 2 * HEAD), bf16)], (states,))
    attention = exchange(attention, "w")
    width = D // (NW * NX)
    terms = call(
        output_kernel,
        [((NX, tok_rows, width), f32)],
        (meta, attention, out_own, out_other),
        scalars=1,
        flops=2 * 64 * 4096 * 288,
    )
    terms = exchange(terms, "x")
    residual = lax.dynamic_slice_in_dim(tokens, fsdp_index * width, width, 1)
    return call(last_kernel, [((tok_rows, width), bf16)], (terms, residual))


def solution(mesh):
    fine = Mesh(mesh.devices.reshape(NZ, NY, NC, NW, NX), SEQ + FSDP)
    return jax.shard_map(
        on_device,
        mesh=fine,
        in_specs=(
            P(SEQ, None),
            P(),
            P(SEQ, FSDP),
            P(FSDP, SEQ),
            P(SEQ, FSDP),
            P(SEQ, FSDP),
            P(),
        ),
        out_specs=P(SEQ, FSDP),
        check_vma=False,
    )
```

```python
import jax
import jax.numpy as jnp
from jax import lax
from jax.experimental import pallas as pl
from jax.experimental.pallas import tpu as pltpu
from jax.sharding import Mesh, PartitionSpec as P

D = 4608
HEAD = 128
HEADS = 32
NZ, NY, NC, NW, NX = 4, 4, 2, 4, 4
SEQ = ("z", "y", "c")
FSDP = ("w", "x")

masked_score = -1e30
epsilon = 1e-06
VMEM_BYTES = 40 * 1024 * 1024


def exchange(x, axis):
    return lax.all_to_all(x, axis, 0, 0, tiled=True)


def from_next(x, axis, step, size):
    return lax.ppermute(x, axis, [((i + step) % size, i) for i in range(size)])


def from_pair(x, axis, bit, size):
    return lax.ppermute(x, axis, [(i ^ bit, i) for i in range(size)])


def stack_z(x):
    return jnp.stack([x] + [from_pair(x, "z", k, NZ) for k in range(1, NZ)])


def block_result(query, keys, values, allowed):
    scores = lax.dot_general(
        keys, query, (((1,), (1,)), ((), ())), preferred_element_type=jnp.float32
    )
    scores = jnp.where(allowed, scores, masked_score)
    best = jnp.max(scores, axis=0, keepdims=True)
    weights = jnp.exp(scores - best)
    total = jnp.where(best > 0.5 * masked_score, jnp.sum(weights, axis=0, keepdims=True), 0.0)
    numer = lax.dot_general(
        values,
        weights.astype(jnp.bfloat16),
        (((0,), (0,)), ((), ())),
        preferred_element_type=jnp.float32,
    )
    inverse = 1.0 / jnp.where(total > 0.0, total, 1.0)
    share = (numer * inverse).astype(jnp.bfloat16)
    return best, total, share


def combine(parts):
    highest = parts[0][0]
    for best, _, _ in parts[1:]:
        highest = jnp.maximum(highest, best)
    denom = 0.0
    accum = 0.0
    for best, total, share in parts:
        weight = total * jnp.exp(best - highest)
        denom = denom + weight
        accum = accum + weight * share.astype(jnp.float32)
    return highest, denom, accum


def norm_kernel(meta, tokens_ref, gain_ref, out_ref, normed_ref):
    hidden = tokens_ref[...].astype(jnp.float32)
    mean = jnp.mean(hidden * hidden, axis=-1, keepdims=True)
    normed_ref[...] = (hidden * lax.rsqrt(mean + epsilon) * gain_ref[...]).astype(jnp.bfloat16)
    span = normed_ref.shape[1] // NZ
    k_rows = span // (NY * NC)
    for k in range(NZ):
        block = meta[1] ^ k
        part = normed_ref[:, pl.ds(pl.multiple_of(block * span, span), span)]
        for i in range(NY * NC):
            piece = part[:, i * k_rows : (i + 1) * k_rows]
            out_ref[i, :, k * k_rows : (k + 1) * k_rows] = piece


def project_kernel(rows_ref, w0, w1, w2, w3, out_ref):
    weights = jnp.concatenate([w[...] for w in (w0, w1, w2, w3)], axis=0)
    peers, rows, depth = rows_ref.shape
    total = jnp.dot(
        rows_ref[...].reshape(peers * rows, depth), weights, preferred_element_type=jnp.float32
    )
    out_ref[...] = total.reshape(out_ref.shape)


def rotary_kernel(part_ref, cos_ref, sin_ref, q_ref, new_ref):
    total = part_ref[0]
    for i in range(1, part_ref.shape[0]):
        total = total + part_ref[i]
    cosine, sine_part = cos_ref[...], sin_ref[...]

    def rotated(i):
        u = total[:, i * HEAD : (i + 1) * HEAD]
        return u * cosine + pltpu.roll(u, HEAD // 2, 1) * sine_part

    scale = (D // HEADS) ** (-0.5)
    first = (rotated(0) * scale).astype(jnp.bfloat16)
    second = (rotated(1) * scale).astype(jnp.bfloat16)
    for i in range(NY * NC):
        q_ref[i, :, :HEAD] = first
        q_ref[i, :, HEAD:] = second
    new_ref[:, :HEAD] = rotated(2).astype(jnp.bfloat16)
    new_ref[:, HEAD:] = total[:, 3 * HEAD :].astype(jnp.bfloat16)


def attention_kernel(meta, q_ref, cache_ref, n0, n1, n2, n3, out_ref):
    length, my_z, y, c = meta[0], meta[1], meta[2], meta[3]
    slots, new_slots = cache_ref.shape[1], n0.shape[0]
    rows = q_ref.shape[1]
    lanes = 4 * rows
    slot = lax.broadcasted_iota(jnp.int32, (slots, lanes), 0)
    key = lax.broadcasted_iota(jnp.int32, (new_slots, lanes), 0)
    lane = lax.broadcasted_iota(jnp.int32, (new_slots, lanes), 1)
    row = lax.broadcasted_iota(jnp.int32, (8, 2 * rows), 0)
    blocks = [((my_z ^ k) * NY + y) * NC + c for k in range(NZ)]
    for pair in range(NY):
        query = jnp.concatenate(
            [
                q_ref[2 * pair + i, :, h * HEAD : (h + 1) * HEAD]
                for i in range(NC)
                for h in range(2)
            ],
            axis=0,
        )
        base = (my_z * NY + pair) * NC * rows
        offset = base + jnp.where(lane < 2 * rows, 0, rows) + lane % rows - key
        parts = []
        for k in range(NZ):
            parts.append(
                block_result(
                    query,
                    cache_ref[k, :, :HEAD],
                    cache_ref[k, :, HEAD:],
                    slot < length - blocks[k] * slots,
                )
            )
        for k, new in enumerate((n0, n1, n2, n3)):
            parts.append(
                block_result(
                    query, new[:, :HEAD], new[:, HEAD:], offset >= blocks[k] * new_slots
                )
            )
        highest, denom, accum = combine(parts)
        for i in range(NC):
            part = slice(i * 2 * rows, (i + 1) * 2 * rows)
            out_ref[2 * pair + i, :HEAD, :] = accum[:, part]
            out_ref[2 * pair + i, HEAD:, :] = jnp.where(row == 0, highest[:, part], denom[:, part])


def merge_kernel(state_ref, out_ref):
    rows = out_ref.shape[1]
    bests = [state_ref[i, HEAD : HEAD + 1, :] for i in range(NY * NC)]
    highest = bests[0]
    for best in bests[1:]:
        highest = jnp.maximum(highest, best)
    denom = 0.0
    accum = 0.0
    for i in range(NY * NC):
        scale = jnp.exp(bests[i] - highest)
        denom = denom + state_ref[i, HEAD + 1 : HEAD + 2, :] * scale
        accum = accum + state_ref[i, :HEAD, :] * scale
    attention = jnp.transpose(accum / denom).astype(jnp.bfloat16)
    for i in range(NW * NC):
        out_ref[i, :, :HEAD] = attention[:rows]
        out_ref[i, :, HEAD:] = attention[rows:]


def output_kernel(meta, att_ref, b0, b1, b2, b3, out_ref):
    rows = att_ref.shape[1]
    att = [
        att_ref[pl.ds((meta[1] ^ k) * NC, NC)].reshape(NC * rows, att_ref.shape[2])
        for k in range(NW)
    ]
    for step, block in enumerate((b0, b1, b2, b3)):
        place = lax.rem(meta[2] + step, NX)
        total = 0.0
        for k in range(NW):
            total = total + lax.dot_general(
                att[k], block[k], (((1,), (1,)), ((), ())), preferred_element_type=jnp.float32
            )
        for i in range(NC):
            out_ref[place * NC + i] = total[i * rows : (i + 1) * rows]


def last_kernel(part_ref, residual_ref, out_ref):
    half = part_ref.shape[2]
    for j in range(NC):
        total = (part_ref[j] + part_ref[NC + j]) + (part_ref[2 * NC + j] + part_ref[3 * NC + j])
        at = slice(j * half, (j + 1) * half)
        out_ref[:, at] = (residual_ref[:, at].astype(jnp.float32) + total).astype(jnp.bfloat16)


def call(kernel, out, operands, scalars=0, flops=0, scratch=(), held=()):
    count, extra = len(operands), len(held)

    def body(*refs):
        after = count + extra
        kernel(*refs[:count], *refs[after : after + len(out)], *refs[after + len(out) + extra :])

    specs = [pl.BlockSpec(memory_space=pltpu.SMEM)] * scalars
    specs += [pl.BlockSpec(memory_space=pltpu.VMEM)] * (count - scalars)
    moved = sum(o.size * o.dtype.itemsize for o in operands)
    shapes = [jax.ShapeDtypeStruct(shape, dtype) for shape, dtype in out]
    shapes += [jax.ShapeDtypeStruct(h.shape, h.dtype) for h in held]
    results = pl.pallas_call(
        body,
        out_shape=shapes,
        in_specs=specs + [pl.BlockSpec(memory_space=pl.ANY)] * extra,
        out_specs=[pl.BlockSpec(memory_space=pltpu.VMEM)] * len(out)
        + [pl.BlockSpec(memory_space=pl.ANY)] * extra,
        scratch_shapes=list(scratch),
        input_output_aliases={count + i: len(out) + i for i in range(extra)},
        compiler_params=pltpu.CompilerParams(vmem_limit_bytes=VMEM_BYTES),
        cost_estimate=pl.CostEstimate(
            flops=flops, bytes_accessed=moved, transcendentals=flops // 512
        ),
    )(*operands, *held)
    return results if len(results) > 1 else results[0]


def on_device(tokens, pre_gain, w_qkv, w_out, cache_keys, cache_values, cache_len):
    tok_rows = tokens.shape[0]
    k_rows = w_qkv.shape[0]
    bf16, f32 = jnp.bfloat16, jnp.float32
    z, y, c = (lax.axis_index(name) for name in SEQ)
    seq_index = (z * NY + y) * NC + c
    fsdp_index = lax.axis_index("w") * NX + lax.axis_index("x")
    length = cache_len[0]
    meta = jnp.stack([length, z, y, c]).astype(jnp.int32)

    rows_out = call(
        norm_kernel,
        [((NY * NC, tok_rows, NZ * k_rows), bf16)],
        (meta, tokens, pre_gain.reshape(1, -1)),
        scalars=1,
        flops=tokens.size * 6,
        scratch=[pltpu.VMEM(tokens.shape, bf16)],
    )
    rows_in = exchange(rows_out, ("y", "c"))
    weights = [w_qkv] + [from_pair(w_qkv, "z", k, NZ) for k in range(1, NZ)]
    trade = [(a * NW + b, b * NW + a) for a in range(NZ) for b in range(NW)]
    out_block = lax.ppermute(w_out.T, ("z", "w"), trade)
    cache = jnp.concatenate([cache_keys, cache_values], axis=1)
    cache = jnp.stack([cache, from_pair(cache, "z", 1, NZ)])
    partial, cache, out_block = call(
        project_kernel,
        [((NY * NC, tok_rows, w_qkv.shape[1]), f32)],
        (rows_in, *weights),
        flops=2 * 256 * 1152 * 512,
        held=(cache, out_block),
    )
    partial = exchange(partial, ("y", "c"))
    cache = jnp.concatenate([cache, from_pair(cache, "z", 2, NZ)])
    out_pair = jnp.stack([out_block, from_pair(out_block, "z", 1, NZ)])

    half_dim = HEAD // 2
    inverse_freq = 10000.0 ** (-jnp.arange(half_dim, dtype=f32) / half_dim)
    positions = length + seq_index * tok_rows + jnp.arange(tok_rows, dtype=jnp.int32)
    angles = positions.astype(f32)[:, None] * inverse_freq[None, :]
    cosine, sine_part = jnp.cos(angles), jnp.sin(angles)
    cosine = jnp.concatenate([cosine, cosine], axis=1)
    sine_part = jnp.concatenate([-sine_part, sine_part], axis=1)
    queries, new, out_pair = call(
        rotary_kernel,
        [((NY * NC, tok_rows, 2 * HEAD), bf16), ((tok_rows, 2 * HEAD), bf16)],
        (partial, cosine, sine_part),
        held=(out_pair,),
    )
    all_queries = exchange(queries, ("y", "c"))
    all_new = [new] + [from_pair(new, "z", k, NZ) for k in range(1, NZ)]
    out_z = jnp.concatenate([out_pair, from_pair(out_pair, "z", 2, NZ)])

    state, out_z = call(
        attention_kernel,
        [((NY * NC, HEAD + 8, 2 * tok_rows), f32)],
        (meta, all_queries, cache, *all_new),
        scalars=1,
        flops=4 * 512 * 2560 * 128,
        held=(out_z,),
    )
    states = exchange(state, ("y", "c"))
    out_weights = [out_z] + [from_next(out_z, "y", k, NY) for k in range(1, NY)]
    attention = call(merge_kernel, [((NW * NC, tok_rows, 2 * HEAD), bf16)], (states,))
    attention = exchange(attention, ("w", "c"))
    width = D // (NW * NX)
    terms = call(
        output_kernel,
        [((NX * NC, tok_rows, width // NC), f32)],
        (meta, attention, *out_weights),
        scalars=1,
        flops=2 * 64 * 4096 * 288,
    )
    terms = exchange(terms, ("x", "c"))
    residual = lax.dynamic_slice_in_dim(tokens, fsdp_index * width, width, 1)
    return call(last_kernel, [((tok_rows, width), bf16)], (terms, residual))


def solution(mesh):
    fine = Mesh(mesh.devices.reshape(NZ, NY, NC, NW, NX), SEQ + FSDP)
    return jax.shard_map(
        on_device,
        mesh=fine,
        in_specs=(
            P(SEQ, None),
            P(),
            P(SEQ, FSDP),
            P(FSDP, SEQ),
            P(SEQ, FSDP),
            P(SEQ, FSDP),
            P(),
        ),
        out_specs=P(SEQ, FSDP),
        check_vma=False,
    )
```

```python
import jax
import jax.numpy as jnp
from jax import lax
from jax.experimental import pallas as pl
from jax.experimental.pallas import tpu as pltpu
from jax.sharding import Mesh, PartitionSpec as P

D = 4608
HEAD = 128
HEADS = 32
NZ, NY, NC, NW, NX = 4, 4, 2, 4, 4
SEQ = ("z", "y", "c")
FSDP = ("w", "x")

masked_score = -1e30
epsilon = 1e-06
VMEM_BYTES = 40 * 1024 * 1024


def swap_core(x):
    return lax.ppermute(x, "c", [(0, 1), (1, 0)])


PAIRS = (0, 2, 1, 3)


def exchange(x, axis):
    return lax.all_to_all(x, axis, 0, 0, tiled=True)


def copies(x, count):
    return jnp.broadcast_to(x[None], (count,) + x.shape)


def from_next(x, axis, step, size):
    return lax.ppermute(x, axis, [((i + step) % size, i) for i in range(size)])


def from_pair(x, axis, bit, size):
    return lax.ppermute(x, axis, [(i ^ bit, i) for i in range(size)])


def block_result(query, keys, values, allowed):
    scores = lax.dot_general(
        keys, query, (((1,), (1,)), ((), ())), preferred_element_type=jnp.float32
    )
    scores = jnp.where(allowed, scores, masked_score)
    best = jnp.max(scores, axis=0, keepdims=True)
    weights = jnp.exp(scores - best)
    total = jnp.where(best > 0.5 * masked_score, jnp.sum(weights, axis=0, keepdims=True), 0.0)
    numer = lax.dot_general(
        values,
        weights.astype(jnp.bfloat16),
        (((0,), (0,)), ((), ())),
        preferred_element_type=jnp.float32,
    )
    inverse = 1.0 / jnp.where(total > 0.0, total, 1.0)
    share = (numer * inverse).astype(jnp.bfloat16)
    return best, total, share


def combine(parts):
    highest = parts[0][0]
    for best, _, _ in parts[1:]:
        highest = jnp.maximum(highest, best)
    denom = 0.0
    accum = 0.0
    for best, total, share in parts:
        weight = total * jnp.exp(best - highest)
        denom = denom + weight
        accum = accum + weight * share.astype(jnp.float32)
    return highest, denom, accum


def joint_results(query, keys, values, alloweds):
    count, slots, _ = keys.shape
    scores = lax.dot_general(
        keys.reshape(count * slots, HEAD),
        query,
        (((1,), (1,)), ((), ())),
        preferred_element_type=jnp.float32,
    )
    turned = jnp.concatenate([values[k].T for k in range(count)], axis=1)
    owner = lax.broadcasted_iota(jnp.int32, turned.shape, 1) // slots
    spread = jnp.concatenate(
        [jnp.where(owner == k, turned, 0.0).astype(jnp.bfloat16) for k in range(count)], axis=0
    )
    stats, rounded = [], []
    for k in range(count):
        part = jnp.where(alloweds[k], scores[k * slots : (k + 1) * slots], masked_score)
        best = jnp.max(part, axis=0, keepdims=True)
        weights = jnp.exp(part - best)
        total = jnp.where(best > 0.5 * masked_score, jnp.sum(weights, axis=0, keepdims=True), 0.0)
        stats.append((best, total))
        rounded.append(weights.astype(jnp.bfloat16))
    numer = jnp.dot(spread, jnp.concatenate(rounded, axis=0), preferred_element_type=jnp.float32)
    parts = []
    for k, (best, total) in enumerate(stats):
        inverse = 1.0 / jnp.where(total > 0.0, total, 1.0)
        share = (numer[k * HEAD : (k + 1) * HEAD] * inverse).astype(jnp.bfloat16)
        parts.append((best, total, share))
    return parts


def combine(parts):
    highest = parts[0][0]
    for best, _, _ in parts[1:]:
        highest = jnp.maximum(highest, best)
    denom = 0.0
    accum = 0.0
    for best, total, share in parts:
        weight = total * jnp.exp(best - highest)
        denom = denom + weight
        accum = accum + weight * share.astype(jnp.float32)
    return highest, denom, accum


def norm_kernel(meta, tokens_ref, gain_ref, out_ref, normed_ref):
    hidden = tokens_ref[...].astype(jnp.float32)
    mean = jnp.mean(hidden * hidden, axis=-1, keepdims=True)
    normed_ref[...] = (hidden * lax.rsqrt(mean + epsilon) * gain_ref[...]).astype(jnp.bfloat16)
    span = normed_ref.shape[1] // NZ
    k_rows = span // (NY * NC)
    for k in range(NZ):
        block = meta[1] ^ k
        part = normed_ref[:, pl.ds(pl.multiple_of(block * span, span), span)]
        for y in range(NY):
            piece = part[:, y * NC * k_rows : (y + 1) * NC * k_rows]
            for i in range(NC):
                out_ref[y * NC + i, :, k * NC * k_rows : (k + 1) * NC * k_rows] = piece


def project_kernel(rows_ref, w0, w1, w2, w3, out_ref):
    weights = jnp.concatenate([w[i] for w in (w0, w1, w2, w3) for i in range(NC)], axis=0)
    peers, rows, depth = rows_ref.shape
    total = jnp.dot(
        rows_ref[...].reshape(peers * rows, depth), weights, preferred_element_type=jnp.float32
    )
    out_ref[...] = total.reshape(out_ref.shape)


def rotary_kernel(part_ref, cos_ref, sin_ref, q_ref, new_ref):
    halves = []
    for c in range(NC):
        halves.append((part_ref[c] + part_ref[NC + c]) + (part_ref[2 * NC + c] + part_ref[3 * NC + c]))
    total = jnp.concatenate(halves, axis=1)
    cosine, sine_part = cos_ref[...], sin_ref[...]

    def rotated(i):
        u = total[:, i * HEAD : (i + 1) * HEAD]
        return u * cosine + pltpu.roll(u, HEAD // 2, 1) * sine_part

    scale = (D // HEADS) ** (-0.5)
    first = (rotated(0) * scale).astype(jnp.bfloat16)
    second = (rotated(1) * scale).astype(jnp.bfloat16)
    for i in range(NY * NC):
        q_ref[i, :, :HEAD] = first
        q_ref[i, :, HEAD:] = second
    new_ref[:, :HEAD] = rotated(2).astype(jnp.bfloat16)
    new_ref[:, HEAD:] = total[:, 3 * HEAD :].astype(jnp.bfloat16)


def attention_kernel(meta, q_ref, cache_ref, n0, n1, n2, n3, out_ref):
    length, my_z, y, c = meta[0], meta[1], meta[2], meta[3]
    slots, new_slots = cache_ref.shape[1], n0.shape[0]
    rows = q_ref.shape[1]
    count = 4
    lanes = count * 2 * rows
    slot = lax.broadcasted_iota(jnp.int32, (slots, lanes), 0)
    key = lax.broadcasted_iota(jnp.int32, (new_slots, lanes), 0)
    lane = lax.broadcasted_iota(jnp.int32, (new_slots, lanes), 1)
    row = lax.broadcasted_iota(jnp.int32, (8, 2 * rows), 0)
    cached = [((my_z ^ k) * NY + y) * NC + c for k in PAIRS]
    fresh = [((my_z ^ k) * NY + y) * NC + c for k in range(NZ)]
    new = jnp.stack([n[...] for n in (n0, n1, n2, n3)])
    for first in range(0, NY * NC, count):
        query = jnp.concatenate(
            [
                q_ref[first + i, :, h * HEAD : (h + 1) * HEAD]
                for i in range(count)
                for h in range(2)
            ],
            axis=0,
        )
        base = (my_z * NY * NC + first) * rows
        offset = base + lane // (2 * rows) * rows + lane % rows - key
        parts = []
        for k in range(NZ):
            parts.append(
                block_result(
                    query,
                    cache_ref[k, :, :HEAD],
                    cache_ref[k, :, HEAD:],
                    slot < length - cached[k] * slots,
                )
            )
        parts += joint_results(
            query,
            new[:, :, :HEAD],
            new[:, :, HEAD:],
            [offset >= at * new_slots for at in fresh],
        )
        highest, denom, accum = combine(parts)
        for i in range(count):
            part = slice(i * 2 * rows, (i + 1) * 2 * rows)
            out_ref[first + i, :HEAD, :] = accum[:, part]
            out_ref[first + i, HEAD:, :] = jnp.where(row == 0, highest[:, part], denom[:, part])


def merge_kernel(state_ref, out_ref):
    rows = out_ref.shape[0]
    bests = [state_ref[i, HEAD : HEAD + 1, :] for i in range(NY * NC)]
    highest = bests[0]
    for best in bests[1:]:
        highest = jnp.maximum(highest, best)
    denom = 0.0
    accum = 0.0
    for i in range(NY * NC):
        scale = jnp.exp(bests[i] - highest)
        denom = denom + state_ref[i, HEAD + 1 : HEAD + 2, :] * scale
        accum = accum + state_ref[i, :HEAD, :] * scale
    attention = jnp.transpose(accum / denom).astype(jnp.bfloat16)
    out_ref[:, :HEAD] = attention[:rows]
    out_ref[:, HEAD:] = attention[rows:]


def output_kernel(meta, att_ref, other_ref, weight_ref, out_ref):
    rows = att_ref.shape[1]
    z, c, w = meta[1], meta[3], meta[4]
    places = [lax.rem((z ^ k) + NW - w, NW) for k in range(NZ)]
    att = [jnp.concatenate([att_ref[at], other_ref[at]], axis=0) for at in places]
    for x in range(NX):
        place = x * NC
        total = 0.0
        for k in range(NW):
            total = total + lax.dot_general(
                att[k],
                weight_ref[x, k],
                (((1,), (1,)), ((), ())),
                preferred_element_type=jnp.float32,
            )
        rest = total[:, HEAD:]
        for i, core in enumerate((c, 1 - c)):
            out_ref[place + core, :rows] = total[i * rows : (i + 1) * rows, :HEAD]
            out_ref[place + core, rows:] = jnp.concatenate(
                [rest[i * rows + g * 8 : i * rows + g * 8 + 8] for g in range(rows // 8)], axis=1
            )


def last_kernel(part_ref, residual_ref, out_ref):
    rows = out_ref.shape[0]
    half = out_ref.shape[1] // NC
    wide = half - HEAD
    for j in range(NC):
        total = (part_ref[j] + part_ref[NC + j]) + (part_ref[2 * NC + j] + part_ref[3 * NC + j])
        rest = total[rows:]
        rest = jnp.concatenate(
            [rest[:, g * wide : (g + 1) * wide] for g in range(rows // 8)], axis=0
        )
        total = jnp.concatenate([total[:rows], rest], axis=1)
        at = slice(j * half, (j + 1) * half)
        out_ref[:, at] = (residual_ref[:, at].astype(jnp.float32) + total).astype(jnp.bfloat16)


def call(kernel, out, operands, scalars=0, flops=0, scratch=(), held=()):
    count, extra = len(operands), len(held)

    def body(*refs):
        after = count + extra
        kernel(*refs[:count], *refs[after : after + len(out)], *refs[after + len(out) + extra :])

    specs = [pl.BlockSpec(memory_space=pltpu.SMEM)] * scalars
    specs += [pl.BlockSpec(memory_space=pltpu.VMEM)] * (count - scalars)
    moved = sum(o.size * o.dtype.itemsize for o in operands)
    shapes = [jax.ShapeDtypeStruct(shape, dtype) for shape, dtype in out]
    shapes += [jax.ShapeDtypeStruct(h.shape, h.dtype) for h in held]
    results = pl.pallas_call(
        body,
        out_shape=shapes,
        in_specs=specs + [pl.BlockSpec(memory_space=pl.ANY)] * extra,
        out_specs=[pl.BlockSpec(memory_space=pltpu.VMEM)] * len(out)
        + [pl.BlockSpec(memory_space=pl.ANY)] * extra,
        scratch_shapes=list(scratch),
        input_output_aliases={count + i: len(out) + i for i in range(extra)},
        compiler_params=pltpu.CompilerParams(vmem_limit_bytes=VMEM_BYTES),
        cost_estimate=pl.CostEstimate(
            flops=flops, bytes_accessed=moved, transcendentals=flops // 512
        ),
    )(*operands, *held)
    return results if len(results) > 1 else results[0]


def on_device(tokens, pre_gain, w_qkv, w_out, cache_keys, cache_values, cache_len):
    tok_rows = tokens.shape[0]
    k_rows = w_qkv.shape[0]
    bf16, f32 = jnp.bfloat16, jnp.float32
    z, y, c = (lax.axis_index(name) for name in SEQ)
    seq_index = (z * NY + y) * NC + c
    fsdp_index = lax.axis_index("w") * NX + lax.axis_index("x")
    length = cache_len[0]
    meta = jnp.stack([length, z, y, c, lax.axis_index("w")]).astype(jnp.int32)

    half = w_qkv.shape[1] // NC
    low, high = w_qkv[:, :half], w_qkv[:, half:]
    kept, given = jnp.where(c == 0, low, high), jnp.where(c == 0, high, low)
    got = swap_core(given)
    w_pair = jnp.where(c == 0, jnp.stack([kept, got]), jnp.stack([got, kept]))
    rows_out = call(
        norm_kernel,
        [((NY * NC, tok_rows, NZ * NC * k_rows), bf16)],
        (meta, tokens, pre_gain.reshape(1, -1)),
        scalars=1,
        flops=tokens.size * 6,
        scratch=[pltpu.VMEM(tokens.shape, bf16)],
    )
    rows_in = exchange(rows_out, ("y", "c"))
    weights = [w_pair] + [from_pair(w_pair, "z", k, NZ) for k in range(1, NZ)]
    trade = [(a * NW + b, b * NW + a) for a in range(NZ) for b in range(NW)]
    out_block = lax.ppermute(w_out.T, ("z", "w"), trade)
    cache = jnp.concatenate([cache_keys, cache_values], axis=1)
    cache = jnp.stack([cache, from_pair(cache, "z", 2, NZ)])
    partial, cache = call(
        project_kernel,
        [((NY * NC, tok_rows, half), f32)],
        (rows_in, *weights),
        flops=2 * 256 * 1152 * 512,
        held=(cache,),
    )
    partial = exchange(partial, ("y", "c"))
    cache = jnp.concatenate([cache, from_pair(cache, "z", 1, NZ)])
    half_dim = HEAD // 2
    inverse_freq = 10000.0 ** (-jnp.arange(half_dim, dtype=f32) / half_dim)
    positions = length + seq_index * tok_rows + jnp.arange(tok_rows, dtype=jnp.int32)
    angles = positions.astype(f32)[:, None] * inverse_freq[None, :]
    cosine, sine_part = jnp.cos(angles), jnp.sin(angles)
    cosine = jnp.concatenate([cosine, cosine], axis=1)
    sine_part = jnp.concatenate([-sine_part, sine_part], axis=1)
    queries, new, out_block = call(
        rotary_kernel,
        [((NY * NC, tok_rows, 2 * HEAD), bf16), ((tok_rows, 2 * HEAD), bf16)],
        (partial, cosine, sine_part),
        held=(out_block,),
    )
    all_queries = exchange(queries, ("y", "c"))
    all_new = [new] + [from_pair(new, "z", k, NZ) for k in range(1, NZ)]

    state, out_block = call(
        attention_kernel,
        [((NY * NC, HEAD + 8, 2 * tok_rows), f32)],
        (meta, all_queries, cache, *all_new),
        scalars=1,
        flops=4 * 512 * 2560 * 128,
        held=(out_block,),
    )
    states = exchange(state, ("y", "c"))
    out_z = jnp.stack([out_block] + [from_pair(out_block, "z", k, NZ) for k in range(1, NZ)])
    attention, out_z = call(
        merge_kernel, [((tok_rows, 2 * HEAD), bf16)], (states,), held=(out_z,)
    )
    out_weights = exchange(copies(out_z, NY), "y")
    attention = jnp.stack([attention] + [from_next(attention, "w", k, NW) for k in range(1, NW)])
    att_other = swap_core(attention)
    width = D // (NW * NX)
    terms = call(
        output_kernel,
        [((NX * NC, tok_rows * width // NC // HEAD, HEAD), f32)],
        (meta, attention, att_other, out_weights),
        scalars=1,
        flops=2 * 64 * 4096 * 288,
    )
    terms = exchange(terms, ("x", "c"))
    residual = lax.dynamic_slice_in_dim(tokens, fsdp_index * width, width, 1)
    return call(last_kernel, [((tok_rows, width), bf16)], (terms, residual))


def solution(mesh):
    fine = Mesh(mesh.devices.reshape(NZ, NY, NC, NW, NX), SEQ + FSDP)
    return jax.shard_map(
        on_device,
        mesh=fine,
        in_specs=(
            P(SEQ, None),
            P(),
            P(SEQ, FSDP),
            P(FSDP, SEQ),
            P(SEQ, FSDP),
            P(SEQ, FSDP),
            P(),
        ),
        out_specs=P(SEQ, FSDP),
        check_vma=False,
    )
```

```python
import jax
import jax.numpy as jnp
from jax import lax
from jax.experimental import pallas as pl
from jax.experimental.pallas import tpu as pltpu
from jax.sharding import Mesh, PartitionSpec as P

D = 4608
HEAD = 128
HEADS = 32
NZ, NY, NC, NW, NX = 4, 4, 2, 4, 4
SEQ = ("z", "y", "c")
FSDP = ("w", "x")

masked_score = -1e30
epsilon = 1e-06
VMEM_BYTES = 40 * 1024 * 1024


def swap_core(x):
    return lax.ppermute(x, "c", [(0, 1), (1, 0)])


PAIRS = (0, 2, 1, 3)


def exchange(x, axis):
    return lax.all_to_all(x, axis, 0, 0, tiled=True)


def copies(x, count):
    return jnp.broadcast_to(x[None], (count,) + x.shape)


def from_next(x, axis, step, size):
    return lax.ppermute(x, axis, [((i + step) % size, i) for i in range(size)])


def from_pair(x, axis, bit, size):
    return lax.ppermute(x, axis, [(i ^ bit, i) for i in range(size)])


def block_result(query, keys, values, allowed):
    scores = lax.dot_general(
        keys, query, (((1,), (1,)), ((), ())), preferred_element_type=jnp.float32
    )
    scores = jnp.where(allowed, scores, masked_score)
    best = jnp.max(scores, axis=0, keepdims=True)
    weights = jnp.exp(scores - best)
    total = jnp.where(best > 0.5 * masked_score, jnp.sum(weights, axis=0, keepdims=True), 0.0)
    numer = lax.dot_general(
        values,
        weights.astype(jnp.bfloat16),
        (((0,), (0,)), ((), ())),
        preferred_element_type=jnp.float32,
    )
    inverse = 1.0 / jnp.where(total > 0.0, total, 1.0)
    share = (numer * inverse).astype(jnp.bfloat16)
    return best, total, share


def combine(parts):
    highest = parts[0][0]
    for best, _, _ in parts[1:]:
        highest = jnp.maximum(highest, best)
    denom = 0.0
    accum = 0.0
    for best, total, share in parts:
        weight = total * jnp.exp(best - highest)
        denom = denom + weight
        accum = accum + weight * share.astype(jnp.float32)
    return highest, denom, accum


def joint_results(query, keys, values, alloweds):
    count, slots, _ = keys.shape
    scores = lax.dot_general(
        keys.reshape(count * slots, HEAD),
        query,
        (((1,), (1,)), ((), ())),
        preferred_element_type=jnp.float32,
    )
    turned = jnp.concatenate([values[k].T for k in range(count)], axis=1)
    owner = lax.broadcasted_iota(jnp.int32, turned.shape, 1) // slots
    spread = jnp.concatenate(
        [jnp.where(owner == k, turned, 0.0).astype(jnp.bfloat16) for k in range(count)], axis=0
    )
    stats, rounded = [], []
    for k in range(count):
        part = jnp.where(alloweds[k], scores[k * slots : (k + 1) * slots], masked_score)
        best = jnp.max(part, axis=0, keepdims=True)
        weights = jnp.exp(part - best)
        total = jnp.where(best > 0.5 * masked_score, jnp.sum(weights, axis=0, keepdims=True), 0.0)
        stats.append((best, total))
        rounded.append(weights.astype(jnp.bfloat16))
    numer = jnp.dot(spread, jnp.concatenate(rounded, axis=0), preferred_element_type=jnp.float32)
    parts = []
    for k, (best, total) in enumerate(stats):
        inverse = 1.0 / jnp.where(total > 0.0, total, 1.0)
        share = (numer[k * HEAD : (k + 1) * HEAD] * inverse).astype(jnp.bfloat16)
        parts.append((best, total, share))
    return parts


def combine(parts):
    highest = parts[0][0]
    for best, _, _ in parts[1:]:
        highest = jnp.maximum(highest, best)
    denom = 0.0
    accum = 0.0
    for best, total, share in parts:
        weight = total * jnp.exp(best - highest)
        denom = denom + weight
        accum = accum + weight * share.astype(jnp.float32)
    return highest, denom, accum


def norm_kernel(meta, tokens_ref, gain_ref, out_ref, normed_ref):
    hidden = tokens_ref[...].astype(jnp.float32)
    mean = jnp.mean(hidden * hidden, axis=-1, keepdims=True)
    normed_ref[...] = (hidden * lax.rsqrt(mean + epsilon) * gain_ref[...]).astype(jnp.bfloat16)
    span = normed_ref.shape[1] // NZ
    k_rows = span // (NY * NC)
    for k in range(NZ):
        block = meta[1] ^ k
        part = normed_ref[:, pl.ds(pl.multiple_of(block * span, span), span)]
        for y in range(NY):
            piece = part[:, y * NC * k_rows : (y + 1) * NC * k_rows]
            for i in range(NC):
                out_ref[y * NC + i, :, k * NC * k_rows : (k + 1) * NC * k_rows] = piece


def project_kernel(rows_ref, w0, w1, w2, w3, out_ref):
    weights = jnp.concatenate([w[i] for w in (w0, w1, w2, w3) for i in range(NC)], axis=0)
    peers, rows, depth = rows_ref.shape
    total = jnp.dot(
        rows_ref[...].reshape(peers * rows, depth), weights, preferred_element_type=jnp.float32
    )
    out_ref[...] = total.reshape(out_ref.shape)


def rotary_kernel(part_ref, cos_ref, sin_ref, q_ref, new_ref):
    halves = []
    for c in range(NC):
        halves.append((part_ref[c] + part_ref[NC + c]) + (part_ref[2 * NC + c] + part_ref[3 * NC + c]))
    total = jnp.concatenate(halves, axis=1)
    cosine, sine_part = cos_ref[...], sin_ref[...]

    def rotated(i):
        u = total[:, i * HEAD : (i + 1) * HEAD]
        return u * cosine + pltpu.roll(u, HEAD // 2, 1) * sine_part

    scale = (D // HEADS) ** (-0.5)
    first = (rotated(0) * scale).astype(jnp.bfloat16)
    second = (rotated(1) * scale).astype(jnp.bfloat16)
    for i in range(NY * NC):
        q_ref[i, :, :HEAD] = first
        q_ref[i, :, HEAD:] = second
    new_ref[:, :HEAD] = rotated(2).astype(jnp.bfloat16)
    new_ref[:, HEAD:] = total[:, 3 * HEAD :].astype(jnp.bfloat16)


def attention_kernel(meta, q_ref, cache_ref, new, out_ref):
    length, my_z, y, c = meta[0], meta[1], meta[2], meta[3]
    slots, new_slots = cache_ref.shape[1], new.shape[1]
    rows = q_ref.shape[1]
    count = 4
    lanes = count * 2 * rows
    slot = lax.broadcasted_iota(jnp.int32, (slots, lanes), 0)
    key = lax.broadcasted_iota(jnp.int32, (new_slots, lanes), 0)
    lane = lax.broadcasted_iota(jnp.int32, (new_slots, lanes), 1)
    row = lax.broadcasted_iota(jnp.int32, (8, 2 * rows), 0)
    cached = [((my_z ^ k) * NY + y) * NC + c for k in PAIRS]
    fresh = [((my_z ^ k) * NY + y) * NC + c for k in PAIRS]
    for first in range(0, NY * NC, count):
        query = jnp.concatenate(
            [
                q_ref[first + i, :, h * HEAD : (h + 1) * HEAD]
                for i in range(count)
                for h in range(2)
            ],
            axis=0,
        )
        base = (my_z * NY * NC + first) * rows
        offset = base + lane // (2 * rows) * rows + lane % rows - key
        parts = []
        for k in range(NZ):
            parts.append(
                block_result(
                    query,
                    cache_ref[k, :, :HEAD],
                    cache_ref[k, :, HEAD:],
                    slot < length - cached[k] * slots,
                )
            )
        parts += joint_results(
            query,
            new[:, :, :HEAD],
            new[:, :, HEAD:],
            [offset >= at * new_slots for at in fresh],
        )
        highest, denom, accum = combine(parts)
        for i in range(count):
            part = slice(i * 2 * rows, (i + 1) * 2 * rows)
            out_ref[first + i, :HEAD, :] = accum[:, part]
            out_ref[first + i, HEAD:, :] = jnp.where(row == 0, highest[:, part], denom[:, part])


def merge_kernel(state_ref, out_ref):
    rows = out_ref.shape[0]
    bests = [state_ref[i, HEAD : HEAD + 1, :] for i in range(NY * NC)]
    highest = bests[0]
    for best in bests[1:]:
        highest = jnp.maximum(highest, best)
    denom = 0.0
    accum = 0.0
    for i in range(NY * NC):
        scale = jnp.exp(bests[i] - highest)
        denom = denom + state_ref[i, HEAD + 1 : HEAD + 2, :] * scale
        accum = accum + state_ref[i, :HEAD, :] * scale
    attention = jnp.transpose(accum / denom).astype(jnp.bfloat16)
    out_ref[:, :HEAD] = attention[:rows]
    out_ref[:, HEAD:] = attention[rows:]


def output_kernel(meta, att_ref, other_ref, weight_ref, out_ref):
    rows = att_ref.shape[1]
    z, c, w = meta[1], meta[3], meta[4]
    places = [lax.rem((z ^ k) + NW - w, NW) for k in range(NZ)]
    att = [jnp.concatenate([att_ref[at], other_ref[at]], axis=0) for at in places]
    for x in range(NX):
        place = x * NC
        total = 0.0
        for k in range(NW):
            total = total + lax.dot_general(
                att[k],
                weight_ref[x, k],
                (((1,), (1,)), ((), ())),
                preferred_element_type=jnp.float32,
            )
        rest = total[:, HEAD:]
        for i, core in enumerate((c, 1 - c)):
            out_ref[place + core, :rows] = total[i * rows : (i + 1) * rows, :HEAD]
            out_ref[place + core, rows:] = jnp.concatenate(
                [rest[i * rows + g * 8 : i * rows + g * 8 + 8] for g in range(rows // 8)], axis=1
            )


def last_kernel(part_ref, residual_ref, out_ref):
    rows = out_ref.shape[0]
    half = out_ref.shape[1] // NC
    wide = half - HEAD
    for j in range(NC):
        total = (part_ref[j] + part_ref[NC + j]) + (part_ref[2 * NC + j] + part_ref[3 * NC + j])
        rest = total[rows:]
        rest = jnp.concatenate(
            [rest[:, g * wide : (g + 1) * wide] for g in range(rows // 8)], axis=0
        )
        total = jnp.concatenate([total[:rows], rest], axis=1)
        at = slice(j * half, (j + 1) * half)
        out_ref[:, at] = (residual_ref[:, at].astype(jnp.float32) + total).astype(jnp.bfloat16)


def call(kernel, out, operands, scalars=0, flops=0, scratch=(), held=()):
    count, extra = len(operands), len(held)

    def body(*refs):
        after = count + extra
        kernel(*refs[:count], *refs[after : after + len(out)], *refs[after + len(out) + extra :])

    specs = [pl.BlockSpec(memory_space=pltpu.SMEM)] * scalars
    specs += [pl.BlockSpec(memory_space=pltpu.VMEM)] * (count - scalars)
    moved = sum(o.size * o.dtype.itemsize for o in operands)
    shapes = [jax.ShapeDtypeStruct(shape, dtype) for shape, dtype in out]
    shapes += [jax.ShapeDtypeStruct(h.shape, h.dtype) for h in held]
    results = pl.pallas_call(
        body,
        out_shape=shapes,
        in_specs=specs + [pl.BlockSpec(memory_space=pl.ANY)] * extra,
        out_specs=[pl.BlockSpec(memory_space=pltpu.VMEM)] * len(out)
        + [pl.BlockSpec(memory_space=pl.ANY)] * extra,
        scratch_shapes=list(scratch),
        input_output_aliases={count + i: len(out) + i for i in range(extra)},
        compiler_params=pltpu.CompilerParams(vmem_limit_bytes=VMEM_BYTES),
        cost_estimate=pl.CostEstimate(
            flops=flops, bytes_accessed=moved, transcendentals=flops // 512
        ),
    )(*operands, *held)
    return results if len(results) > 1 else results[0]


def on_device(tokens, pre_gain, w_qkv, w_out, cache_keys, cache_values, cache_len):
    tok_rows = tokens.shape[0]
    k_rows = w_qkv.shape[0]
    bf16, f32 = jnp.bfloat16, jnp.float32
    z, y, c = (lax.axis_index(name) for name in SEQ)
    seq_index = (z * NY + y) * NC + c
    fsdp_index = lax.axis_index("w") * NX + lax.axis_index("x")
    length = cache_len[0]
    meta = jnp.stack([length, z, y, c, lax.axis_index("w")]).astype(jnp.int32)

    half = w_qkv.shape[1] // NC
    low, high = w_qkv[:, :half], w_qkv[:, half:]
    kept, given = jnp.where(c == 0, low, high), jnp.where(c == 0, high, low)
    got = swap_core(given)
    w_pair = jnp.where(c == 0, jnp.stack([kept, got]), jnp.stack([got, kept]))
    rows_out = call(
        norm_kernel,
        [((NY * NC, tok_rows, NZ * NC * k_rows), bf16)],
        (meta, tokens, pre_gain.reshape(1, -1)),
        scalars=1,
        flops=tokens.size * 6,
        scratch=[pltpu.VMEM(tokens.shape, bf16)],
    )
    rows_in = exchange(rows_out, ("y", "c"))
    weights = [w_pair] + [from_pair(w_pair, "z", k, NZ) for k in range(1, NZ)]
    trade = [(a * NW + b, b * NW + a) for a in range(NZ) for b in range(NW)]
    out_block = lax.ppermute(w_out.T, ("z", "w"), trade)
    cache = jnp.concatenate([cache_keys, cache_values], axis=1)
    cache = jnp.stack([cache, from_pair(cache, "z", 2, NZ)])
    partial, cache = call(
        project_kernel,
        [((NY * NC, tok_rows, half), f32)],
        (rows_in, *weights),
        flops=2 * 256 * 1152 * 512,
        held=(cache,),
    )
    partial = exchange(partial, ("y", "c"))
    cache = jnp.concatenate([cache, from_pair(cache, "z", 1, NZ)])
    half_dim = HEAD // 2
    inverse_freq = 10000.0 ** (-jnp.arange(half_dim, dtype=f32) / half_dim)
    positions = length + seq_index * tok_rows + jnp.arange(tok_rows, dtype=jnp.int32)
    angles = positions.astype(f32)[:, None] * inverse_freq[None, :]
    cosine, sine_part = jnp.cos(angles), jnp.sin(angles)
    cosine = jnp.concatenate([cosine, cosine], axis=1)
    sine_part = jnp.concatenate([-sine_part, sine_part], axis=1)
    queries, new, out_block = call(
        rotary_kernel,
        [((NY * NC, tok_rows, 2 * HEAD), bf16), ((tok_rows, 2 * HEAD), bf16)],
        (partial, cosine, sine_part),
        held=(out_block,),
    )
    all_queries = exchange(queries, ("y", "c"))
    all_new = jnp.stack([new, from_pair(new, "z", 2, NZ)])
    all_new = jnp.concatenate([all_new, from_pair(all_new, "z", 1, NZ)])

    state, out_block = call(
        attention_kernel,
        [((NY * NC, HEAD + 8, 2 * tok_rows), f32)],
        (meta, all_queries, cache, all_new),
        scalars=1,
        flops=4 * 512 * 2560 * 128,
        held=(out_block,),
    )
    states = exchange(state, ("y", "c"))
    out_z = jnp.stack([out_block] + [from_pair(out_block, "z", k, NZ) for k in range(1, NZ)])
    attention, out_z = call(
        merge_kernel, [((tok_rows, 2 * HEAD), bf16)], (states,), held=(out_z,)
    )
    out_weights = exchange(copies(out_z, NY), "y")
    attention = jnp.stack([attention] + [from_next(attention, "w", k, NW) for k in range(1, NW)])
    att_other = swap_core(attention)
    width = D // (NW * NX)
    terms = call(
        output_kernel,
        [((NX * NC, tok_rows * width // NC // HEAD, HEAD), f32)],
        (meta, attention, att_other, out_weights),
        scalars=1,
        flops=2 * 64 * 4096 * 288,
    )
    terms = exchange(terms, ("x", "c"))
    residual = lax.dynamic_slice_in_dim(tokens, fsdp_index * width, width, 1)
    return call(last_kernel, [((tok_rows, width), bf16)], (terms, residual))


def solution(mesh):
    fine = Mesh(mesh.devices.reshape(NZ, NY, NC, NW, NX), SEQ + FSDP)
    return jax.shard_map(
        on_device,
        mesh=fine,
        in_specs=(
            P(SEQ, None),
            P(),
            P(SEQ, FSDP),
            P(FSDP, SEQ),
            P(SEQ, FSDP),
            P(SEQ, FSDP),
            P(),
        ),
        out_specs=P(SEQ, FSDP),
        check_vma=False,
    )
```

```python
import jax
import jax.numpy as jnp
from jax import lax
from jax.experimental import pallas as pl
from jax.experimental.pallas import tpu as pltpu
from jax.sharding import Mesh, PartitionSpec as P

D = 4608
HEAD = 128
HEADS = 32
NZ, NY, NC, NW, NX = 4, 4, 2, 4, 4
SEQ = ("z", "y", "c")
FSDP = ("w", "x")

masked_score = -1e30
epsilon = 1e-06
VMEM_BYTES = 40 * 1024 * 1024


def swap_core(x):
    return lax.ppermute(x, "c", [(0, 1), (1, 0)])


PAIRS = (0, 2, 1, 3)


def exchange(x, axis):
    return lax.all_to_all(x, axis, 0, 0, tiled=True)


def copies(x, count):
    return jnp.broadcast_to(x[None], (count,) + x.shape)


def from_next(x, axis, step, size):
    return lax.ppermute(x, axis, [((i + step) % size, i) for i in range(size)])


def from_pair(x, axis, bit, size):
    return lax.ppermute(x, axis, [(i ^ bit, i) for i in range(size)])


def block_result(query, keys, values, allowed):
    scores = lax.dot_general(
        keys, query, (((1,), (1,)), ((), ())), preferred_element_type=jnp.float32
    )
    scores = jnp.where(allowed, scores, masked_score)
    best = jnp.max(scores, axis=0, keepdims=True)
    weights = jnp.exp(scores - best)
    total = jnp.where(best > 0.5 * masked_score, jnp.sum(weights, axis=0, keepdims=True), 0.0)
    numer = lax.dot_general(
        values,
        weights.astype(jnp.bfloat16),
        (((0,), (0,)), ((), ())),
        preferred_element_type=jnp.float32,
    )
    inverse = 1.0 / jnp.where(total > 0.0, total, 1.0)
    share = (numer * inverse).astype(jnp.bfloat16)
    return best, total, share


def combine(parts):
    highest = parts[0][0]
    for best, _, _ in parts[1:]:
        highest = jnp.maximum(highest, best)
    denom = 0.0
    accum = 0.0
    for best, total, share in parts:
        weight = total * jnp.exp(best - highest)
        denom = denom + weight
        accum = accum + weight * share.astype(jnp.float32)
    return highest, denom, accum


def joint_results(query, keys, values, alloweds):
    count, slots, _ = keys.shape
    scores = lax.dot_general(
        keys.reshape(count * slots, HEAD),
        query,
        (((1,), (1,)), ((), ())),
        preferred_element_type=jnp.float32,
    )
    turned = jnp.concatenate([values[k].T for k in range(count)], axis=1)
    owner = lax.broadcasted_iota(jnp.int32, turned.shape, 1) // slots
    spread = jnp.concatenate(
        [jnp.where(owner == k, turned, 0.0).astype(jnp.bfloat16) for k in range(count)], axis=0
    )
    stats, rounded = [], []
    for k in range(count):
        part = jnp.where(alloweds[k], scores[k * slots : (k + 1) * slots], masked_score)
        best = jnp.max(part, axis=0, keepdims=True)
        weights = jnp.exp(part - best)
        total = jnp.where(best > 0.5 * masked_score, jnp.sum(weights, axis=0, keepdims=True), 0.0)
        stats.append((best, total))
        rounded.append(weights.astype(jnp.bfloat16))
    numer = jnp.dot(spread, jnp.concatenate(rounded, axis=0), preferred_element_type=jnp.float32)
    parts = []
    for k, (best, total) in enumerate(stats):
        inverse = 1.0 / jnp.where(total > 0.0, total, 1.0)
        share = (numer[k * HEAD : (k + 1) * HEAD] * inverse).astype(jnp.bfloat16)
        parts.append((best, total, share))
    return parts


def combine(parts):
    highest = parts[0][0]
    for best, _, _ in parts[1:]:
        highest = jnp.maximum(highest, best)
    denom = 0.0
    accum = 0.0
    for best, total, share in parts:
        weight = total * jnp.exp(best - highest)
        denom = denom + weight
        accum = accum + weight * share.astype(jnp.float32)
    return highest, denom, accum


def norm_kernel(meta, tokens_ref, gain_ref, out_ref, normed_ref):
    hidden = tokens_ref[...].astype(jnp.float32)
    mean = jnp.mean(hidden * hidden, axis=-1, keepdims=True)
    normed_ref[...] = (hidden * lax.rsqrt(mean + epsilon) * gain_ref[...]).astype(jnp.bfloat16)
    span = normed_ref.shape[1] // NZ
    k_rows = span // (NY * NC)
    for k in range(NZ):
        block = meta[1] ^ k
        part = normed_ref[:, pl.ds(pl.multiple_of(block * span, span), span)]
        for y in range(NY):
            piece = part[:, y * NC * k_rows : (y + 1) * NC * k_rows]
            for i in range(NC):
                out_ref[y * NC + i, :, k * NC * k_rows : (k + 1) * NC * k_rows] = piece


def project_kernel(rows_ref, w0, w1, w2, w3, out_ref):
    weights = jnp.concatenate([w[i] for w in (w0, w1, w2, w3) for i in range(NC)], axis=0)
    peers, rows, depth = rows_ref.shape
    total = jnp.dot(
        rows_ref[...].reshape(peers * rows, depth), weights, preferred_element_type=jnp.float32
    )
    out_ref[...] = total.reshape(out_ref.shape)


def rotary_kernel(part_ref, cos_ref, sin_ref, q_ref, new_ref):
    halves = []
    for c in range(NC):
        halves.append((part_ref[c] + part_ref[NC + c]) + (part_ref[2 * NC + c] + part_ref[3 * NC + c]))
    total = jnp.concatenate(halves, axis=1)
    cosine, sine_part = cos_ref[...], sin_ref[...]

    def rotated(i):
        u = total[:, i * HEAD : (i + 1) * HEAD]
        return u * cosine + pltpu.roll(u, HEAD // 2, 1) * sine_part

    scale = (D // HEADS) ** (-0.5)
    first = (rotated(0) * scale).astype(jnp.bfloat16)
    second = (rotated(1) * scale).astype(jnp.bfloat16)
    for i in range(NY * NC):
        q_ref[i, :, :HEAD] = first
        q_ref[i, :, HEAD:] = second
    new_ref[:, :HEAD] = rotated(2).astype(jnp.bfloat16)
    new_ref[:, HEAD:] = total[:, 3 * HEAD :].astype(jnp.bfloat16)


def attention_kernel(meta, q_ref, cache_ref, new, out_ref):
    length, my_z, y, c = meta[0], meta[1], meta[2], meta[3]
    slots, new_slots = cache_ref.shape[1], new.shape[1]
    rows = q_ref.shape[1]
    count = 4
    lanes = count * 2 * rows
    slot = lax.broadcasted_iota(jnp.int32, (slots, lanes), 0)
    key = lax.broadcasted_iota(jnp.int32, (new_slots, lanes), 0)
    lane = lax.broadcasted_iota(jnp.int32, (new_slots, lanes), 1)
    row = lax.broadcasted_iota(jnp.int32, (8, 2 * rows), 0)
    cached = [((my_z ^ k) * NY + y) * NC + c for k in PAIRS]
    fresh = [((my_z ^ k) * NY + y) * NC + c for k in PAIRS]
    for first in range(0, NY * NC, count):
        query = jnp.concatenate(
            [
                q_ref[first + i, :, h * HEAD : (h + 1) * HEAD]
                for i in range(count)
                for h in range(2)
            ],
            axis=0,
        )
        base = (my_z * NY * NC + first) * rows
        offset = base + lane // (2 * rows) * rows + lane % rows - key
        parts = []
        for k in range(NZ):
            parts.append(
                block_result(
                    query,
                    cache_ref[k, :, :HEAD],
                    cache_ref[k, :, HEAD:],
                    slot < length - cached[k] * slots,
                )
            )
        parts += joint_results(
            query,
            new[:, :, :HEAD],
            new[:, :, HEAD:],
            [offset >= at * new_slots for at in fresh],
        )
        highest, denom, accum = combine(parts)
        for i in range(count):
            part = slice(i * 2 * rows, (i + 1) * 2 * rows)
            out_ref[first + i, :HEAD, :] = accum[:, part]
            out_ref[first + i, HEAD:, :] = jnp.where(row == 0, highest[:, part], denom[:, part])


def merge_kernel(state_ref, block_ref, out_ref, copies_ref):
    for i in range(NY):
        copies_ref[i] = block_ref[...]
    rows = out_ref.shape[0]
    bests = [state_ref[i, HEAD : HEAD + 1, :] for i in range(NY * NC)]
    highest = bests[0]
    for best in bests[1:]:
        highest = jnp.maximum(highest, best)
    denom = 0.0
    accum = 0.0
    for i in range(NY * NC):
        scale = jnp.exp(bests[i] - highest)
        denom = denom + state_ref[i, HEAD + 1 : HEAD + 2, :] * scale
        accum = accum + state_ref[i, :HEAD, :] * scale
    attention = jnp.transpose(accum / denom).astype(jnp.bfloat16)
    out_ref[:, :HEAD] = attention[:rows]
    out_ref[:, HEAD:] = attention[rows:]


def output_kernel(meta, att_ref, other_ref, weight_ref, out_ref):
    rows = att_ref.shape[1]
    half = weight_ref.shape[2] // 2
    z, c, w = meta[1], meta[3], meta[4]
    steps = [lax.rem((z ^ k) + NW - w, NW) for k in PAIRS]
    places = [jnp.where(step < 2, step, 5 - step) for step in steps]
    att = [jnp.concatenate([att_ref[at], other_ref[at]], axis=0) for at in places]
    for x in range(NX):
        total = 0.0
        for k in range(NW):
            total = total + lax.dot_general(
                weight_ref[x, k],
                att[k],
                (((1,), (1,)), ((), ())),
                preferred_element_type=jnp.float32,
            )
        for i, core in enumerate((c, 1 - c)):
            part = total[:, i * rows : (i + 1) * rows]
            out_ref[x * NC + core] = jnp.concatenate([part[:half], part[half:]], axis=1)


def last_kernel(part_ref, residual_ref, out_ref):
    rows = out_ref.shape[0]
    columns = []
    for j in range(NC):
        total = (part_ref[j] + part_ref[NC + j]) + (part_ref[2 * NC + j] + part_ref[3 * NC + j])
        columns += [total[:, :rows], total[:, rows:]]
    total = jnp.transpose(jnp.concatenate(columns, axis=0))
    out_ref[...] = (residual_ref[...].astype(jnp.float32) + total).astype(jnp.bfloat16)


def call(kernel, out, operands, scalars=0, flops=0, scratch=(), held=()):
    count, extra = len(operands), len(held)

    def body(*refs):
        after = count + extra
        kernel(*refs[:count], *refs[after : after + len(out)], *refs[after + len(out) + extra :])

    specs = [pl.BlockSpec(memory_space=pltpu.SMEM)] * scalars
    specs += [pl.BlockSpec(memory_space=pltpu.VMEM)] * (count - scalars)
    moved = sum(o.size * o.dtype.itemsize for o in operands)
    shapes = [jax.ShapeDtypeStruct(shape, dtype) for shape, dtype in out]
    shapes += [jax.ShapeDtypeStruct(h.shape, h.dtype) for h in held]
    results = pl.pallas_call(
        body,
        out_shape=shapes,
        in_specs=specs + [pl.BlockSpec(memory_space=pl.ANY)] * extra,
        out_specs=[pl.BlockSpec(memory_space=pltpu.VMEM)] * len(out)
        + [pl.BlockSpec(memory_space=pl.ANY)] * extra,
        scratch_shapes=list(scratch),
        input_output_aliases={count + i: len(out) + i for i in range(extra)},
        compiler_params=pltpu.CompilerParams(vmem_limit_bytes=VMEM_BYTES),
        cost_estimate=pl.CostEstimate(
            flops=flops, bytes_accessed=moved, transcendentals=flops // 512
        ),
    )(*operands, *held)
    return results if len(results) > 1 else results[0]


def on_device(tokens, pre_gain, w_qkv, w_out, cache_keys, cache_values, cache_len):
    tok_rows = tokens.shape[0]
    k_rows = w_qkv.shape[0]
    bf16, f32 = jnp.bfloat16, jnp.float32
    z, y, c = (lax.axis_index(name) for name in SEQ)
    seq_index = (z * NY + y) * NC + c
    fsdp_index = lax.axis_index("w") * NX + lax.axis_index("x")
    length = cache_len[0]
    meta = jnp.stack([length, z, y, c, lax.axis_index("w")]).astype(jnp.int32)

    half = w_qkv.shape[1] // NC
    low, high = w_qkv[:, :half], w_qkv[:, half:]
    kept, given = jnp.where(c == 0, low, high), jnp.where(c == 0, high, low)
    got = swap_core(given)
    w_pair = jnp.where(c == 0, jnp.stack([kept, got]), jnp.stack([got, kept]))
    rows_out = call(
        norm_kernel,
        [((NY * NC, tok_rows, NZ * NC * k_rows), bf16)],
        (meta, tokens, pre_gain.reshape(1, -1)),
        scalars=1,
        flops=tokens.size * 6,
        scratch=[pltpu.VMEM(tokens.shape, bf16)],
    )
    rows_in = exchange(rows_out, ("y", "c"))
    weights = [w_pair] + [from_pair(w_pair, "z", k, NZ) for k in range(1, NZ)]
    trade = [(a * NW + b, b * NW + a) for a in range(NZ) for b in range(NW)]
    out_block = lax.ppermute(w_out.T, ("z", "w"), trade)
    cache = jnp.concatenate([cache_keys, cache_values], axis=1)
    cache = jnp.stack([cache, from_pair(cache, "z", 2, NZ)])
    partial, cache = call(
        project_kernel,
        [((NY * NC, tok_rows, half), f32)],
        (rows_in, *weights),
        flops=2 * 256 * 1152 * 512,
        held=(cache,),
    )
    partial = exchange(partial, ("y", "c"))
    cache = jnp.concatenate([cache, from_pair(cache, "z", 1, NZ)])
    half_dim = HEAD // 2
    inverse_freq = 10000.0 ** (-jnp.arange(half_dim, dtype=f32) / half_dim)
    positions = length + seq_index * tok_rows + jnp.arange(tok_rows, dtype=jnp.int32)
    angles = positions.astype(f32)[:, None] * inverse_freq[None, :]
    cosine, sine_part = jnp.cos(angles), jnp.sin(angles)
    cosine = jnp.concatenate([cosine, cosine], axis=1)
    sine_part = jnp.concatenate([-sine_part, sine_part], axis=1)
    queries, new, out_block = call(
        rotary_kernel,
        [((NY * NC, tok_rows, 2 * HEAD), bf16), ((tok_rows, 2 * HEAD), bf16)],
        (partial, cosine, sine_part),
        held=(out_block,),
    )
    all_queries = exchange(queries, ("y", "c"))
    all_new = jnp.stack([new, from_pair(new, "z", 2, NZ)])
    all_new = jnp.concatenate([all_new, from_pair(all_new, "z", 1, NZ)])

    out_pair = jnp.stack([out_block, from_pair(out_block, "z", 2, NZ)])
    state, out_pair = call(
        attention_kernel,
        [((NY * NC, HEAD + 8, 2 * tok_rows), f32)],
        (meta, all_queries, cache, all_new),
        scalars=1,
        flops=4 * 512 * 2560 * 128,
        held=(out_pair,),
    )
    states = exchange(state, ("y", "c"))
    out_z = jnp.concatenate([out_pair, from_pair(out_pair, "z", 1, NZ)])
    attention, out_copies = call(
        merge_kernel,
        [((tok_rows, 2 * HEAD), bf16), ((NY,) + out_z.shape, bf16)],
        (states, out_z),
    )
    out_weights = exchange(out_copies, "y")
    attention = jnp.stack([attention] + [from_next(attention, "w", k, NW) for k in (1, 3, 2)])
    att_other = swap_core(attention)
    width = D // (NW * NX)
    terms = call(
        output_kernel,
        [((NX * NC, tok_rows * width // NC // HEAD, HEAD), f32)],
        (meta, attention, att_other, out_weights),
        scalars=1,
        flops=2 * 64 * 4096 * 288,
    )
    terms = exchange(terms, ("x", "c"))
    residual = lax.dynamic_slice_in_dim(tokens, fsdp_index * width, width, 1)
    return call(last_kernel, [((tok_rows, width), bf16)], (terms, residual))


def solution(mesh):
    fine = Mesh(mesh.devices.reshape(NZ, NY, NC, NW, NX), SEQ + FSDP)
    return jax.shard_map(
        on_device,
        mesh=fine,
        in_specs=(
            P(SEQ, None),
            P(),
            P(SEQ, FSDP),
            P(FSDP, SEQ),
            P(SEQ, FSDP),
            P(SEQ, FSDP),
            P(),
        ),
        out_specs=P(SEQ, FSDP),
        check_vma=False,
    )
```

```python
import jax
import jax.numpy as jnp
from jax import lax
from jax.experimental import pallas as pl
from jax.experimental.pallas import tpu as pltpu
from jax.sharding import Mesh, PartitionSpec as P

D = 4608
HEAD = 128
HEADS = 32
NZ, NY, NC, NW, NX = 4, 4, 2, 4, 4
SEQ = ("z", "y", "c")
FSDP = ("w", "x")

masked_score = -1e30
epsilon = 1e-06
VMEM_BYTES = 40 * 1024 * 1024


def swap_core(x):
    return lax.ppermute(x, "c", [(0, 1), (1, 0)])


PAIRS = (0, 2, 1, 3)


def exchange(x, axis):
    return lax.all_to_all(x, axis, 0, 0, tiled=True)


def copies(x, count):
    return jnp.broadcast_to(x[None], (count,) + x.shape)


def from_next(x, axis, step, size):
    return lax.ppermute(x, axis, [((i + step) % size, i) for i in range(size)])


def from_pair(x, axis, bit, size):
    return lax.ppermute(x, axis, [(i ^ bit, i) for i in range(size)])


def block_result(query, keys, values, allowed):
    scores = lax.dot_general(
        keys, query, (((1,), (1,)), ((), ())), preferred_element_type=jnp.float32
    )
    scores = jnp.where(allowed, scores, masked_score)
    best = jnp.max(scores, axis=0, keepdims=True)
    weights = jnp.exp(scores - best)
    total = jnp.where(best > 0.5 * masked_score, jnp.sum(weights, axis=0, keepdims=True), 0.0)
    numer = lax.dot_general(
        values,
        weights.astype(jnp.bfloat16),
        (((0,), (0,)), ((), ())),
        preferred_element_type=jnp.float32,
    )
    inverse = 1.0 / jnp.where(total > 0.0, total, 1.0)
    share = (numer * inverse).astype(jnp.bfloat16)
    return best, total, share


def combine(parts):
    highest = parts[0][0]
    for best, _, _ in parts[1:]:
        highest = jnp.maximum(highest, best)
    denom = 0.0
    accum = 0.0
    for best, total, share in parts:
        weight = total * jnp.exp(best - highest)
        denom = denom + weight
        accum = accum + weight * share.astype(jnp.float32)
    return highest, denom, accum


def joint_results(query, keys, values, alloweds):
    count, slots, _ = keys.shape
    scores = lax.dot_general(
        keys.reshape(count * slots, HEAD),
        query,
        (((1,), (1,)), ((), ())),
        preferred_element_type=jnp.float32,
    )
    turned = jnp.concatenate([values[k].T for k in range(count)], axis=1)
    owner = lax.broadcasted_iota(jnp.int32, turned.shape, 1) // slots
    spread = jnp.concatenate(
        [jnp.where(owner == k, turned, 0.0).astype(jnp.bfloat16) for k in range(count)], axis=0
    )
    stats, rounded = [], []
    for k in range(count):
        part = jnp.where(alloweds[k], scores[k * slots : (k + 1) * slots], masked_score)
        best = jnp.max(part, axis=0, keepdims=True)
        weights = jnp.exp(part - best)
        total = jnp.where(best > 0.5 * masked_score, jnp.sum(weights, axis=0, keepdims=True), 0.0)
        stats.append((best, total))
        rounded.append(weights.astype(jnp.bfloat16))
    numer = jnp.dot(spread, jnp.concatenate(rounded, axis=0), preferred_element_type=jnp.float32)
    parts = []
    for k, (best, total) in enumerate(stats):
        inverse = 1.0 / jnp.where(total > 0.0, total, 1.0)
        share = (numer[k * HEAD : (k + 1) * HEAD] * inverse).astype(jnp.bfloat16)
        parts.append((best, total, share))
    return parts


def combine(parts):
    highest = parts[0][0]
    for best, _, _ in parts[1:]:
        highest = jnp.maximum(highest, best)
    denom = 0.0
    accum = 0.0
    for best, total, share in parts:
        weight = total * jnp.exp(best - highest)
        denom = denom + weight
        accum = accum + weight * share.astype(jnp.float32)
    return highest, denom, accum


def norm_kernel(meta, tokens_ref, gain_ref, out_ref, normed_ref):
    hidden = tokens_ref[...].astype(jnp.float32)
    mean = jnp.mean(hidden * hidden, axis=-1, keepdims=True)
    normed_ref[...] = (hidden * lax.rsqrt(mean + epsilon) * gain_ref[...]).astype(jnp.bfloat16)
    span = normed_ref.shape[1] // NZ
    k_rows = span // (NY * NC)
    for k in range(NZ):
        block = meta[1] ^ k
        part = normed_ref[:, pl.ds(pl.multiple_of(block * span, span), span)]
        for y in range(NY):
            piece = part[:, y * NC * k_rows : (y + 1) * NC * k_rows]
            for i in range(NC):
                out_ref[y * NC + i, :, k * NC * k_rows : (k + 1) * NC * k_rows] = piece


def project_kernel(rows_ref, w0, w1, w2, w3, out_ref):
    weights = jnp.concatenate([w[i] for w in (w0, w1, w2, w3) for i in range(NC)], axis=0)
    peers, rows, depth = rows_ref.shape
    total = jnp.dot(
        rows_ref[...].reshape(peers * rows, depth), weights, preferred_element_type=jnp.float32
    )
    out_ref[...] = total.reshape(out_ref.shape)


def rotary_kernel(part_ref, cos_ref, sin_ref, q_ref, new_ref):
    halves = []
    for c in range(NC):
        halves.append((part_ref[c] + part_ref[NC + c]) + (part_ref[2 * NC + c] + part_ref[3 * NC + c]))
    total = jnp.concatenate(halves, axis=1)
    cosine, sine_part = cos_ref[...], sin_ref[...]

    def rotated(i):
        u = total[:, i * HEAD : (i + 1) * HEAD]
        return u * cosine + pltpu.roll(u, HEAD // 2, 1) * sine_part

    scale = (D // HEADS) ** (-0.5)
    first = (rotated(0) * scale).astype(jnp.bfloat16)
    second = (rotated(1) * scale).astype(jnp.bfloat16)
    for i in range(NY * NC):
        q_ref[i, :, :HEAD] = first
        q_ref[i, :, HEAD:] = second
    new_ref[:, :HEAD] = rotated(2).astype(jnp.bfloat16)
    new_ref[:, HEAD:] = total[:, 3 * HEAD :].astype(jnp.bfloat16)


def attention_kernel(meta, q_ref, cache_ref, new, out_ref):
    length, my_z, y, c = meta[0], meta[1], meta[2], meta[3]
    slots, new_slots = cache_ref.shape[1], new.shape[1]
    rows = q_ref.shape[1]
    count = 4
    lanes = count * 2 * rows
    slot = lax.broadcasted_iota(jnp.int32, (slots, lanes), 0)
    key = lax.broadcasted_iota(jnp.int32, (new_slots, lanes), 0)
    lane = lax.broadcasted_iota(jnp.int32, (new_slots, lanes), 1)
    row = lax.broadcasted_iota(jnp.int32, (8, 2 * rows), 0)
    cached = [((my_z ^ k) * NY + y) * NC + c for k in PAIRS]
    fresh = [((my_z ^ k) * NY + y) * NC + c for k in PAIRS]
    for first in range(0, NY * NC, count):
        query = jnp.concatenate(
            [
                q_ref[first + i, :, h * HEAD : (h + 1) * HEAD]
                for i in range(count)
                for h in range(2)
            ],
            axis=0,
        )
        base = (my_z * NY * NC + first) * rows
        offset = base + lane // (2 * rows) * rows + lane % rows - key
        parts = []
        for k in range(NZ):
            parts.append(
                block_result(
                    query,
                    cache_ref[k, :, :HEAD],
                    cache_ref[k, :, HEAD:],
                    slot < length - cached[k] * slots,
                )
            )
        parts += joint_results(
            query,
            new[:, :, :HEAD],
            new[:, :, HEAD:],
            [offset >= at * new_slots for at in fresh],
        )
        highest, denom, accum = combine(parts)
        for i in range(count):
            part = slice(i * 2 * rows, (i + 1) * 2 * rows)
            out_ref[first + i, :HEAD, :] = accum[:, part]
            out_ref[first + i, HEAD:, :] = jnp.where(row == 0, highest[:, part], denom[:, part])


def merge_kernel(state_ref, block_ref, out_ref, copies_ref):
    for i in range(NY):
        copies_ref[i] = block_ref[...]
    rows = out_ref.shape[0]
    bests = [state_ref[i, HEAD : HEAD + 1, :] for i in range(NY * NC)]
    highest = bests[0]
    for best in bests[1:]:
        highest = jnp.maximum(highest, best)
    denom = 0.0
    accum = 0.0
    for i in range(NY * NC):
        scale = jnp.exp(bests[i] - highest)
        denom = denom + state_ref[i, HEAD + 1 : HEAD + 2, :] * scale
        accum = accum + state_ref[i, :HEAD, :] * scale
    attention = jnp.transpose(accum / denom).astype(jnp.bfloat16)
    out_ref[:, :HEAD] = attention[:rows]
    out_ref[:, HEAD:] = attention[rows:]


def output_kernel(meta, att_ref, other_ref, weight_ref, out_ref):
    rows = att_ref.shape[1]
    half = weight_ref.shape[2] // 2
    z, c, w = meta[1], meta[3], meta[4]
    steps = [lax.rem((z ^ k) + NW - w, NW) for k in PAIRS]
    places = [jnp.where(step < 2, step, 5 - step) for step in steps]
    att = [jnp.concatenate([att_ref[at], other_ref[at]], axis=0) for at in places]
    for x in range(NX):
        total = 0.0
        for k in range(NW):
            total = total + lax.dot_general(
                weight_ref[x, k],
                att[k],
                (((1,), (1,)), ((), ())),
                preferred_element_type=jnp.float32,
            )
        for i, core in enumerate((c, 1 - c)):
            part = total[:, i * rows : (i + 1) * rows]
            out_ref[x * NC + core] = jnp.concatenate([part[:half], part[half:]], axis=1)


def last_kernel(part_ref, residual_ref, out_ref):
    rows = out_ref.shape[0]
    columns = []
    for j in range(NC):
        total = (part_ref[j] + part_ref[NC + j]) + (part_ref[2 * NC + j] + part_ref[3 * NC + j])
        columns += [total[:, :rows], total[:, rows:]]
    total = jnp.transpose(jnp.concatenate(columns, axis=0))
    out_ref[...] = (residual_ref[...].astype(jnp.float32) + total).astype(jnp.bfloat16)


def call(kernel, out, operands, scalars=0, flops=0, scratch=(), held=()):
    count, extra = len(operands), len(held)

    def body(*refs):
        after = count + extra
        kernel(*refs[:count], *refs[after : after + len(out)], *refs[after + len(out) + extra :])

    specs = [pl.BlockSpec(memory_space=pltpu.SMEM)] * scalars
    specs += [pl.BlockSpec(memory_space=pltpu.VMEM)] * (count - scalars)
    moved = sum(o.size * o.dtype.itemsize for o in operands)
    shapes = [jax.ShapeDtypeStruct(shape, dtype) for shape, dtype in out]
    shapes += [jax.ShapeDtypeStruct(h.shape, h.dtype) for h in held]
    results = pl.pallas_call(
        body,
        out_shape=shapes,
        in_specs=specs + [pl.BlockSpec(memory_space=pl.ANY)] * extra,
        out_specs=[pl.BlockSpec(memory_space=pltpu.VMEM)] * len(out)
        + [pl.BlockSpec(memory_space=pl.ANY)] * extra,
        scratch_shapes=list(scratch),
        input_output_aliases={count + i: len(out) + i for i in range(extra)},
        compiler_params=pltpu.CompilerParams(vmem_limit_bytes=VMEM_BYTES),
        cost_estimate=pl.CostEstimate(
            flops=flops, bytes_accessed=moved, transcendentals=flops // 512
        ),
    )(*operands, *held)
    return results if len(results) > 1 else results[0]


def on_device(tokens, pre_gain, w_qkv, w_out, cache_keys, cache_values, cache_len):
    tok_rows = tokens.shape[0]
    k_rows = w_qkv.shape[0]
    bf16, f32 = jnp.bfloat16, jnp.float32
    z, y, c = (lax.axis_index(name) for name in SEQ)
    seq_index = (z * NY + y) * NC + c
    fsdp_index = lax.axis_index("w") * NX + lax.axis_index("x")
    length = cache_len[0]
    meta = jnp.stack([length, z, y, c, lax.axis_index("w")]).astype(jnp.int32)

    half = w_qkv.shape[1] // NC
    low, high = w_qkv[:, :half], w_qkv[:, half:]
    kept, given = jnp.where(c == 0, low, high), jnp.where(c == 0, high, low)
    got = swap_core(given)
    w_pair = jnp.where(c == 0, jnp.stack([kept, got]), jnp.stack([got, kept]))
    rows_out = call(
        norm_kernel,
        [((NY * NC, tok_rows, NZ * NC * k_rows), bf16)],
        (meta, tokens, pre_gain.reshape(1, -1)),
        scalars=1,
        flops=tokens.size * 6,
        scratch=[pltpu.VMEM(tokens.shape, bf16)],
    )
    rows_in = exchange(rows_out, ("y", "c"))
    weights = [w_pair] + [from_pair(w_pair, "z", k, NZ) for k in range(1, NZ)]
    trade = [(a * NW + b, b * NW + a) for a in range(NZ) for b in range(NW)]
    out_block = lax.ppermute(w_out.T, ("z", "w"), trade)
    cache = jnp.concatenate([cache_keys, cache_values], axis=1)
    cache = jnp.stack([cache, from_pair(cache, "z", 2, NZ)])
    partial, cache = call(
        project_kernel,
        [((NY * NC, tok_rows, half), f32)],
        (rows_in, *weights),
        flops=2 * 256 * 1152 * 512,
        held=(cache,),
    )
    partial = exchange(partial, ("y", "c"))
    cache = jnp.concatenate([cache, from_pair(cache, "z", 1, NZ)])
    half_dim = HEAD // 2
    inverse_freq = 10000.0 ** (-jnp.arange(half_dim, dtype=f32) / half_dim)
    positions = length + seq_index * tok_rows + jnp.arange(tok_rows, dtype=jnp.int32)
    angles = positions.astype(f32)[:, None] * inverse_freq[None, :]
    cosine, sine_part = jnp.cos(angles), jnp.sin(angles)
    cosine = jnp.concatenate([cosine, cosine], axis=1)
    sine_part = jnp.concatenate([-sine_part, sine_part], axis=1)
    queries, new = call(
        rotary_kernel,
        [((NY * NC, tok_rows, 2 * HEAD), bf16), ((tok_rows, 2 * HEAD), bf16)],
        (partial, cosine, sine_part),
    )
    all_queries = exchange(queries, ("y", "c"))
    all_new = jnp.stack([new, from_pair(new, "z", 2, NZ)])
    all_new = jnp.concatenate([all_new, from_pair(all_new, "z", 1, NZ)])

    out_pair = jnp.stack([out_block, from_pair(out_block, "z", 2, NZ)])
    state, out_pair = call(
        attention_kernel,
        [((NY * NC, HEAD + 8, 2 * tok_rows), f32)],
        (meta, all_queries, cache, all_new),
        scalars=1,
        flops=4 * 512 * 2560 * 128,
        held=(out_pair,),
    )
    states = exchange(state, ("y", "c"))
    out_z = jnp.concatenate([out_pair, from_pair(out_pair, "z", 1, NZ)])
    attention, out_copies = call(
        merge_kernel,
        [((tok_rows, 2 * HEAD), bf16), ((NY,) + out_z.shape, bf16)],
        (states, out_z),
    )
    out_weights = exchange(out_copies, "y")
    attention = jnp.stack([attention] + [from_next(attention, "w", k, NW) for k in (1, 3, 2)])
    att_other = swap_core(attention)
    width = D // (NW * NX)
    terms = call(
        output_kernel,
        [((NX * NC, tok_rows * width // NC // HEAD, HEAD), f32)],
        (meta, attention, att_other, out_weights),
        scalars=1,
        flops=2 * 64 * 4096 * 288,
    )
    terms = exchange(terms, ("x", "c"))
    residual = lax.dynamic_slice_in_dim(tokens, fsdp_index * width, width, 1)
    return call(last_kernel, [((tok_rows, width), bf16)], (terms, residual))


def solution(mesh):
    fine = Mesh(mesh.devices.reshape(NZ, NY, NC, NW, NX), SEQ + FSDP)
    return jax.shard_map(
        on_device,
        mesh=fine,
        in_specs=(
            P(SEQ, None),
            P(),
            P(SEQ, FSDP),
            P(FSDP, SEQ),
            P(SEQ, FSDP),
            P(SEQ, FSDP),
            P(),
        ),
        out_specs=P(SEQ, FSDP),
        check_vma=False,
    )
```

```python
import jax
import jax.numpy as jnp
from jax import lax
from jax.experimental import pallas as pl
from jax.experimental.pallas import tpu as pltpu
from jax.sharding import Mesh, PartitionSpec as P

D = 4608
HEAD = 128
HEADS = 32
NZ, NY, NC, NW, NX = 4, 4, 2, 4, 4
SEQ = ("z", "y", "c")
FSDP = ("w", "x")

masked_score = -1e30
epsilon = 1e-06
VMEM_BYTES = 40 * 1024 * 1024


def swap_core(x):
    return lax.ppermute(x, "c", [(0, 1), (1, 0)])


PAIRS = (0, 2, 1, 3)


def exchange(x, axis):
    return lax.all_to_all(x, axis, 0, 0, tiled=True)


def copies(x, count):
    return jnp.broadcast_to(x[None], (count,) + x.shape)


def from_next(x, axis, step, size):
    return lax.ppermute(x, axis, [((i + step) % size, i) for i in range(size)])


def from_pair(x, axis, bit, size):
    return lax.ppermute(x, axis, [(i ^ bit, i) for i in range(size)])


def block_result(query, keys, values, allowed):
    scores = lax.dot_general(
        keys, query, (((1,), (1,)), ((), ())), preferred_element_type=jnp.float32
    )
    scores = jnp.where(allowed, scores, masked_score)
    best = jnp.max(scores, axis=0, keepdims=True)
    weights = jnp.exp(scores - best)
    total = jnp.where(best > 0.5 * masked_score, jnp.sum(weights, axis=0, keepdims=True), 0.0)
    numer = lax.dot_general(
        values,
        weights.astype(jnp.bfloat16),
        (((0,), (0,)), ((), ())),
        preferred_element_type=jnp.float32,
    )
    inverse = 1.0 / jnp.where(total > 0.0, total, 1.0)
    share = (numer * inverse).astype(jnp.bfloat16)
    return best, total, share


def combine(parts):
    highest = parts[0][0]
    for best, _, _ in parts[1:]:
        highest = jnp.maximum(highest, best)
    denom = 0.0
    accum = 0.0
    for best, total, share in parts:
        weight = total * jnp.exp(best - highest)
        denom = denom + weight
        accum = accum + weight * share.astype(jnp.float32)
    return highest, denom, accum


def joint_results(query, keys, values, alloweds):
    count, slots, _ = keys.shape
    scores = lax.dot_general(
        keys.reshape(count * slots, HEAD),
        query,
        (((1,), (1,)), ((), ())),
        preferred_element_type=jnp.float32,
    )
    turned = jnp.concatenate([values[k].T for k in range(count)], axis=1)
    owner = lax.broadcasted_iota(jnp.int32, turned.shape, 1) // slots
    spread = jnp.concatenate(
        [jnp.where(owner == k, turned, 0.0).astype(jnp.bfloat16) for k in range(count)], axis=0
    )
    stats, rounded = [], []
    for k in range(count):
        part = jnp.where(alloweds[k], scores[k * slots : (k + 1) * slots], masked_score)
        best = jnp.max(part, axis=0, keepdims=True)
        weights = jnp.exp(part - best)
        total = jnp.where(best > 0.5 * masked_score, jnp.sum(weights, axis=0, keepdims=True), 0.0)
        stats.append((best, total))
        rounded.append(weights.astype(jnp.bfloat16))
    numer = jnp.dot(spread, jnp.concatenate(rounded, axis=0), preferred_element_type=jnp.float32)
    parts = []
    for k, (best, total) in enumerate(stats):
        inverse = 1.0 / jnp.where(total > 0.0, total, 1.0)
        share = (numer[k * HEAD : (k + 1) * HEAD] * inverse).astype(jnp.bfloat16)
        parts.append((best, total, share))
    return parts


def combine(parts):
    highest = parts[0][0]
    for best, _, _ in parts[1:]:
        highest = jnp.maximum(highest, best)
    denom = 0.0
    accum = 0.0
    for best, total, share in parts:
        weight = total * jnp.exp(best - highest)
        denom = denom + weight
        accum = accum + weight * share.astype(jnp.float32)
    return highest, denom, accum


def norm_kernel(meta, tokens_ref, gain_ref, out_ref, normed_ref):
    hidden = tokens_ref[...].astype(jnp.float32)
    mean = jnp.mean(hidden * hidden, axis=-1, keepdims=True)
    normed_ref[...] = (hidden * lax.rsqrt(mean + epsilon) * gain_ref[...]).astype(jnp.bfloat16)
    span = normed_ref.shape[1] // NZ
    k_rows = span // (NY * NC)
    for k in range(NZ):
        block = meta[1] ^ k
        part = normed_ref[:, pl.ds(pl.multiple_of(block * span, span), span)]
        for y in range(NY):
            piece = part[:, y * NC * k_rows : (y + 1) * NC * k_rows]
            for i in range(NC):
                out_ref[y * NC + i, :, k * NC * k_rows : (k + 1) * NC * k_rows] = piece


def project_kernel(rows_ref, w0, w1, w2, w3, out_ref):
    weights = jnp.concatenate([w[i] for w in (w0, w1, w2, w3) for i in range(NC)], axis=0)
    peers, rows, depth = rows_ref.shape
    total = jnp.dot(
        rows_ref[...].reshape(peers * rows, depth), weights, preferred_element_type=jnp.float32
    )
    out_ref[...] = total.reshape(out_ref.shape)


def rotary_kernel(part_ref, cos_ref, sin_ref, q_ref, new_ref):
    halves = []
    for c in range(NC):
        halves.append((part_ref[c] + part_ref[NC + c]) + (part_ref[2 * NC + c] + part_ref[3 * NC + c]))
    total = jnp.concatenate(halves, axis=1)
    cosine, sine_part = cos_ref[...], sin_ref[...]

    def rotated(i):
        u = total[:, i * HEAD : (i + 1) * HEAD]
        return u * cosine + pltpu.roll(u, HEAD // 2, 1) * sine_part

    scale = (D // HEADS) ** (-0.5)
    first = (rotated(0) * scale).astype(jnp.bfloat16)
    second = (rotated(1) * scale).astype(jnp.bfloat16)
    for i in range(NY * NC):
        q_ref[i, :, :HEAD] = first
        q_ref[i, :, HEAD:] = second
    new_ref[:, :HEAD] = rotated(2).astype(jnp.bfloat16)
    new_ref[:, HEAD:] = total[:, 3 * HEAD :].astype(jnp.bfloat16)


def attention_kernel(meta, q_ref, cache_ref, new, out_ref):
    length, my_z, y, c = meta[0], meta[1], meta[2], meta[3]
    slots, new_slots = cache_ref.shape[1], new.shape[1]
    rows = q_ref.shape[1]
    count = 4
    lanes = count * 2 * rows
    slot = lax.broadcasted_iota(jnp.int32, (slots, lanes), 0)
    key = lax.broadcasted_iota(jnp.int32, (new_slots, lanes), 0)
    lane = lax.broadcasted_iota(jnp.int32, (new_slots, lanes), 1)
    row = lax.broadcasted_iota(jnp.int32, (8, 2 * rows), 0)
    cached = [((my_z ^ k) * NY + y) * NC + c for k in PAIRS]
    fresh = [((my_z ^ k) * NY + y) * NC + c for k in PAIRS]
    for first in range(0, NY * NC, count):
        query = jnp.concatenate(
            [
                q_ref[first + i, :, h * HEAD : (h + 1) * HEAD]
                for i in range(count)
                for h in range(2)
            ],
            axis=0,
        )
        base = (my_z * NY * NC + first) * rows
        offset = base + lane // (2 * rows) * rows + lane % rows - key
        parts = []
        for k in range(NZ):
            parts.append(
                block_result(
                    query,
                    cache_ref[k, :, :HEAD],
                    cache_ref[k, :, HEAD:],
                    slot < length - cached[k] * slots,
                )
            )
        parts += joint_results(
            query,
            new[:, :, :HEAD],
            new[:, :, HEAD:],
            [offset >= at * new_slots for at in fresh],
        )
        highest, denom, accum = combine(parts)
        for i in range(count):
            part = slice(i * 2 * rows, (i + 1) * 2 * rows)
            out_ref[first + i, :HEAD, :] = accum[:, part]
            out_ref[first + i, HEAD:, :] = jnp.where(row == 0, highest[:, part], denom[:, part])


def merge_kernel(state_ref, block_ref, out_ref, copies_ref):
    for i in range(NY):
        copies_ref[i] = block_ref[...]
    rows = out_ref.shape[0]
    bests = [state_ref[i, HEAD : HEAD + 1, :] for i in range(NY * NC)]
    highest = bests[0]
    for best in bests[1:]:
        highest = jnp.maximum(highest, best)
    denom = 0.0
    accum = 0.0
    for i in range(NY * NC):
        scale = jnp.exp(bests[i] - highest)
        denom = denom + state_ref[i, HEAD + 1 : HEAD + 2, :] * scale
        accum = accum + state_ref[i, :HEAD, :] * scale
    attention = jnp.transpose(accum / denom).astype(jnp.bfloat16)
    out_ref[:, :HEAD] = attention[:rows]
    out_ref[:, HEAD:] = attention[rows:]


def output_kernel(meta, att_ref, other_ref, weight_ref, out_ref):
    rows = att_ref.shape[1]
    half = weight_ref.shape[2] // 2
    z, c, w = meta[1], meta[3], meta[4]
    steps = [lax.rem((z ^ k) + NW - w, NW) for k in PAIRS]
    places = [jnp.where(step < 2, step, 5 - step) for step in steps]
    att = [jnp.concatenate([att_ref[at], other_ref[at]], axis=0) for at in places]
    columns = weight_ref.shape[2]
    total = 0.0
    for k in range(NW):
        total = total + lax.dot_general(
            weight_ref[:, k].reshape(NX * columns, weight_ref.shape[3]),
            att[k],
            (((1,), (1,)), ((), ())),
            preferred_element_type=jnp.float32,
        )
    for x in range(NX):
        for i, core in enumerate((c, 1 - c)):
            part = total[x * columns : (x + 1) * columns, i * rows : (i + 1) * rows]
            out_ref[x * NC + core] = jnp.concatenate([part[:half], part[half:]], axis=1)


def last_kernel(part_ref, residual_ref, out_ref):
    rows = out_ref.shape[0]
    columns = []
    for j in range(NC):
        total = (part_ref[j] + part_ref[NC + j]) + (part_ref[2 * NC + j] + part_ref[3 * NC + j])
        columns += [total[:, :rows], total[:, rows:]]
    total = jnp.transpose(jnp.concatenate(columns, axis=0))
    out_ref[...] = (residual_ref[...].astype(jnp.float32) + total).astype(jnp.bfloat16)


def call(kernel, out, operands, scalars=0, flops=0, scratch=(), held=()):
    count, extra = len(operands), len(held)

    def body(*refs):
        after = count + extra
        kernel(*refs[:count], *refs[after : after + len(out)], *refs[after + len(out) + extra :])

    specs = [pl.BlockSpec(memory_space=pltpu.SMEM)] * scalars
    specs += [pl.BlockSpec(memory_space=pltpu.VMEM)] * (count - scalars)
    moved = sum(o.size * o.dtype.itemsize for o in operands)
    shapes = [jax.ShapeDtypeStruct(shape, dtype) for shape, dtype in out]
    shapes += [jax.ShapeDtypeStruct(h.shape, h.dtype) for h in held]
    results = pl.pallas_call(
        body,
        out_shape=shapes,
        in_specs=specs + [pl.BlockSpec(memory_space=pl.ANY)] * extra,
        out_specs=[pl.BlockSpec(memory_space=pltpu.VMEM)] * len(out)
        + [pl.BlockSpec(memory_space=pl.ANY)] * extra,
        scratch_shapes=list(scratch),
        input_output_aliases={count + i: len(out) + i for i in range(extra)},
        compiler_params=pltpu.CompilerParams(vmem_limit_bytes=VMEM_BYTES),
        cost_estimate=pl.CostEstimate(
            flops=flops, bytes_accessed=moved, transcendentals=flops // 512
        ),
    )(*operands, *held)
    return results if len(results) > 1 else results[0]


def on_device(tokens, pre_gain, w_qkv, w_out, cache_keys, cache_values, cache_len):
    tok_rows = tokens.shape[0]
    k_rows = w_qkv.shape[0]
    bf16, f32 = jnp.bfloat16, jnp.float32
    z, y, c = (lax.axis_index(name) for name in SEQ)
    seq_index = (z * NY + y) * NC + c
    fsdp_index = lax.axis_index("w") * NX + lax.axis_index("x")
    length = cache_len[0]
    meta = jnp.stack([length, z, y, c, lax.axis_index("w")]).astype(jnp.int32)

    half = w_qkv.shape[1] // NC
    low, high = w_qkv[:, :half], w_qkv[:, half:]
    kept, given = jnp.where(c == 0, low, high), jnp.where(c == 0, high, low)
    got = swap_core(given)
    w_pair = jnp.where(c == 0, jnp.stack([kept, got]), jnp.stack([got, kept]))
    rows_out = call(
        norm_kernel,
        [((NY * NC, tok_rows, NZ * NC * k_rows), bf16)],
        (meta, tokens, pre_gain.reshape(1, -1)),
        scalars=1,
        flops=tokens.size * 6,
        scratch=[pltpu.VMEM(tokens.shape, bf16)],
    )
    rows_in = exchange(rows_out, ("y", "c"))
    weights = [w_pair] + [from_pair(w_pair, "z", k, NZ) for k in range(1, NZ)]
    trade = [(a * NW + b, b * NW + a) for a in range(NZ) for b in range(NW)]
    out_block = lax.ppermute(w_out.T, ("z", "w"), trade)
    cache = jnp.concatenate([cache_keys, cache_values], axis=1)
    cache = jnp.stack([cache, from_pair(cache, "z", 2, NZ)])
    partial, cache = call(
        project_kernel,
        [((NY * NC, tok_rows, half), f32)],
        (rows_in, *weights),
        flops=2 * 256 * 1152 * 512,
        held=(cache,),
    )
    partial = exchange(partial, ("y", "c"))
    cache = jnp.concatenate([cache, from_pair(cache, "z", 1, NZ)])
    half_dim = HEAD // 2
    inverse_freq = 10000.0 ** (-jnp.arange(half_dim, dtype=f32) / half_dim)
    positions = length + seq_index * tok_rows + jnp.arange(tok_rows, dtype=jnp.int32)
    angles = positions.astype(f32)[:, None] * inverse_freq[None, :]
    cosine, sine_part = jnp.cos(angles), jnp.sin(angles)
    cosine = jnp.concatenate([cosine, cosine], axis=1)
    sine_part = jnp.concatenate([-sine_part, sine_part], axis=1)
    queries, new = call(
        rotary_kernel,
        [((NY * NC, tok_rows, 2 * HEAD), bf16), ((tok_rows, 2 * HEAD), bf16)],
        (partial, cosine, sine_part),
    )
    all_queries = exchange(queries, ("y", "c"))
    all_new = jnp.stack([new, from_pair(new, "z", 2, NZ)])
    all_new = jnp.concatenate([all_new, from_pair(all_new, "z", 1, NZ)])

    out_pair = jnp.stack([out_block, from_pair(out_block, "z", 2, NZ)])
    state, out_pair = call(
        attention_kernel,
        [((NY * NC, HEAD + 8, 2 * tok_rows), f32)],
        (meta, all_queries, cache, all_new),
        scalars=1,
        flops=4 * 512 * 2560 * 128,
        held=(out_pair,),
    )
    states = exchange(state, ("y", "c"))
    out_z = jnp.concatenate([out_pair, from_pair(out_pair, "z", 1, NZ)])
    attention, out_copies = call(
        merge_kernel,
        [((tok_rows, 2 * HEAD), bf16), ((NY,) + out_z.shape, bf16)],
        (states, out_z),
    )
    out_weights = exchange(out_copies, "y")
    attention = jnp.stack([attention] + [from_next(attention, "w", k, NW) for k in (1, 3, 2)])
    att_other = swap_core(attention)
    width = D // (NW * NX)
    terms = call(
        output_kernel,
        [((NX * NC, tok_rows * width // NC // HEAD, HEAD), f32)],
        (meta, attention, att_other, out_weights),
        scalars=1,
        flops=2 * 64 * 4096 * 288,
    )
    terms = exchange(terms, ("x", "c"))
    residual = lax.dynamic_slice_in_dim(tokens, fsdp_index * width, width, 1)
    return call(last_kernel, [((tok_rows, width), bf16)], (terms, residual))


def solution(mesh):
    fine = Mesh(mesh.devices.reshape(NZ, NY, NC, NW, NX), SEQ + FSDP)
    return jax.shard_map(
        on_device,
        mesh=fine,
        in_specs=(
            P(SEQ, None),
            P(),
            P(SEQ, FSDP),
            P(FSDP, SEQ),
            P(SEQ, FSDP),
            P(SEQ, FSDP),
            P(),
        ),
        out_specs=P(SEQ, FSDP),
        check_vma=False,
    )
```
